32 devices in a mesh: stretch: 4 (over x, core), stream: 8 (over z, y).
Axes of the slice: x: 2, y: 2, z: 4, core: 2. Of those that a mesh axis runs over, the one named last changes fastest.
Arguments:
- inputs: bfloat16 [2, 8, 1024, 2304], P(None, 'stream', 'stretch'), may hold values from -6 to 6
- weight: bfloat16 [4608, 6912], P('stream'), may hold values from -0.09375 to 0.09375
- bias: float32 [6912], replicated, may hold values from -6 to 10
- reset: int32 [2, 8, 1024], P(None, 'stream', 'stretch'), may hold values from 0 to 1
- cotangent: bfloat16 [2, 8, 1024, 2304], P(None, 'stream', 'stretch'), may hold values from -6 to 6
Outputs:
- hidden: bfloat16 [2, 8, 1024, 2304], P(None, 'stream', 'stretch')
- grad_inputs: float32 [2, 8, 1024, 2304], P(None, 'stream', 'stretch')
- grad_weight: float32 [4608, 6912], P('stream')
- grad_bias: float32 [6912], replicated
The draws below stay inside these ranges and needn't reach their ends.
All inputs are finite; a program needn't handle non-finite values.
Results may differ from the reference program's by a relative error of at most 0.0029.
Values may be sent and summed in bfloat16 or wider, within the bound.
No kernel may reach another device: no remote copies, remote signals or barrier semaphores. Data moves between devices by JAX's collectives and lax.ppermute only.
A program may use at most 512 MiB of HBM per device.

```python
import jax
import jax.numpy as jnp
from jax import lax

D = 2304
MB = 2
SEQ = 1024
CH_TOK = 256
STREAMS = 8


def draw_bias(key, part):
    key = jax.random.fold_in(key, 7)
    keys = jax.random.split(key, 5)
    share = 0.5
    cand_part = 0.5 * jax.random.normal(keys[0], (D,), jnp.float32)
    out_part = 0.5 * jax.random.normal(keys[1], (D,), jnp.float32)
    slow = jax.random.uniform(keys[2], (D,), jnp.float32) < share
    slow_bias = jax.random.uniform(keys[3], (D,), jnp.float32, 7.0, 9.5)
    fast_bias = jax.random.uniform(keys[4], (D,), jnp.float32, 1.5, 4.5)
    forget_part = jnp.where(slow, slow_bias, fast_bias)
    return jnp.concatenate([jnp.clip(cand_part, -3.0, 3.0), forget_part, jnp.clip(out_part, -3.0, 3.0)])


def draw_reset(key, part):
    key = jax.random.fold_in(key, 11)
    keys = jax.random.split(key, 5)
    steps = jnp.arange(SEQ)
    scattered = jax.random.randint(keys[0], (MB, STREAMS, SEQ), 0, SEQ) < 6
    picked = jax.random.randint(keys[1], (STREAMS,), 0, MB)
    begin = jax.random.randint(keys[2], (STREAMS,), 1, CH_TOK // 2 + 1)
    finish = jax.random.randint(keys[3], (STREAMS,), SEQ - CH_TOK // 2, SEQ)
    edges = jax.random.randint(keys[4], (MB, STREAMS, SEQ), 0, 4) == 0
    outside = (steps[None, :] < begin[:, None]) | (steps[None, :] >= finish[:, None])
    spanning = edges & outside[None] | (steps[None, None, :] == begin[None, :, None]) | (steps[None, None, :] == finish[None, :, None])
    chosen = jnp.arange(MB)[:, None] == picked[None, :]
    marks = jnp.where(chosen[..., None], spanning, scattered)
    marks = marks | (steps[None, None, :] == 0)
    return marks.astype(jnp.int32)


def block_scale(stream_key, dims, cuts, low, high):
    factor_of = 1.0
    for position, blocks in cuts:
        steps = jax.random.uniform(jax.random.fold_in(jax.random.fold_in(stream_key, 6), position), (blocks,), jnp.float32, low / len(cuts), high / len(cuts))
        factor_of = factor_of * jnp.repeat(jnp.exp(steps), dims[position] // blocks).reshape((-1,) + (1,) * (len(dims) - 1 - position))
    return factor_of


def noise(stream_key, extent, spread, limit, cuts=(), kind=jnp.bfloat16):
    loudness = block_scale(stream_key, extent, cuts, -0.22, 0.18) if cuts else 1.0
    array = jax.random.normal(stream_key, extent, jnp.float32) * spread * loudness
    return jnp.minimum(jnp.maximum(array, -limit), limit).astype(kind)


def setup_inputs(seed: int = 0) -> dict:
    seeds = jax.random.split(jax.random.key(seed), 6)
    inputs = noise(seeds[0], (MB, STREAMS, SEQ, D), 1.0, 6.0, ((1, 8), (2, 4)))
    weight = noise(seeds[1], (2 * D, 3 * D), (2 * D) ** -0.5, 0.09375, ((0, 8),))
    bias = draw_bias(jax.random.fold_in(seeds[5], 71), 0)
    reset = draw_reset(jax.random.fold_in(seeds[5], 71), 0)
    cotangent = noise(seeds[4], (MB, STREAMS, SEQ, D), 1.0, 6.0, ((1, 8), (2, 4)))
    return {"inputs": inputs, "weight": weight, "bias": bias, "reset": reset, "cotangent": cotangent}


@jax.custom_vjp
def low(v):
    return lax.optimization_barrier(v.astype(jnp.bfloat16)).astype(jnp.float32)

@jax.custom_vjp
def low_back(v):
    return v

def low_keep(v):
    return (low(v), None)

def low_pass(kept, grad):
    return (grad,)

def back_keep(v):
    return (v, None)

def back_low(kept, grad):
    return (low(grad),)
low.defvjp(low_keep, low_pass)
low_back.defvjp(back_keep, back_low)

def compose(first, second):
    return (first[0] * second[0], first[1] * second[0] + second[1])

def forward(inputs, weight, bias, keep):
    width = inputs.shape[-1]
    groups = MB * STREAMS // 4
    streams = inputs.reshape(groups, 4, SEQ, width)
    keeps = keep.reshape(groups, 4, SEQ)

    def group_fn(args):
        tokens, kept = args
        before = jnp.concatenate([jnp.zeros_like(tokens[:, :1, :]), tokens[:, :-1, :]], axis=1)
        stacked = jnp.concatenate([tokens, before], axis=2)
        gates = jnp.einsum('gtk,kn->gtn', stacked, weight, precision=lax.Precision.HIGHEST) + bias
        gates = low_back(gates)
        cand = jnp.tanh(gates[..., :width])
        forget = jax.nn.sigmoid(gates[..., width:2 * width])
        outgate = jax.nn.sigmoid(gates[..., 2 * width:])
        decay = forget * kept[..., None]
        inject = (1.0 - forget) * cand
        _, cell = lax.associative_scan(compose, (decay, inject), axis=1)
        return outgate * cell
    result = lax.map(jax.checkpoint(group_fn), (streams, keeps))
    return result.reshape(inputs.shape)

def reference(inputs, weight, bias, reset, cotangent):
    keep = 1.0 - reset.astype(jnp.float32)

    def run(a, w, b):
        return forward(a, w, b, keep)
    hidden, pull = jax.vjp(run, inputs.astype(jnp.float32), weight.astype(jnp.float32), bias)
    grad_inputs, grad_weight, grad_bias = pull(cotangent.astype(jnp.float32))
    return (hidden.astype(jnp.bfloat16), grad_inputs, grad_weight, grad_bias)
```

```python
import functools

import jax
import jax.numpy as jnp
from jax import lax
from jax.experimental import pallas as pl
from jax.experimental.pallas import tpu as pltpu
from jax.sharding import PartitionSpec as P

BF = jnp.bfloat16
F32 = jnp.float32
LANES = 128
VMEM_BYTES = 60 * 1024 * 1024


def any_spec():
    return pl.BlockSpec(memory_space=pl.ANY)


def vmem_spec():
    return pl.BlockSpec(memory_space=pltpu.VMEM)


def smem_spec():
    return pl.BlockSpec(memory_space=pltpu.SMEM)


def ring_order(count):
    inner = 1
    while (2 * inner) ** 2 <= count:
        inner *= 2
    outer = count // inner
    if inner == 1 or outer % 2:
        return list(range(count))
    order = [z * inner for z in range(outer)]
    for turn, z in enumerate(reversed(range(outer))):
        across = range(1, inner) if turn % 2 == 0 else reversed(range(1, inner))
        order += [z * inner + y for y in across]
    return order


def sigmoid(v):
    return 0.5 + 0.5 * jnp.tanh(0.5 * v)


def gates_kernel(rows, half, n_blocks, n_pieces, group, ids, *refs):
    x_refs = refs[:n_blocks]
    own_ref = refs[n_blocks]
    w_refs = refs[n_blocks + 1 : n_blocks + 1 + n_pieces]
    bias_ref, keep_ref, cot_ref = refs[n_blocks + 1 + n_pieces : n_blocks + 4 + n_pieces]
    hid_ref, dg_ref, db_ref = refs[n_blocks + 4 + n_pieces : n_blocks + 7 + n_pieces]
    x_buf, w_buf, gate_buf, cell_buf, adj_buf, x_sem, w_sem = refs[n_blocks + 7 + n_pieces :]
    time, width = x_buf.shape
    cols = gate_buf.shape[1]
    tile = w_buf.shape[2]
    batch = ids[0]

    def x_copy(i):
        start = pl.multiple_of(ids[1 + i] * rows, rows)
        return pltpu.make_async_copy(x_refs[i].at[batch], x_buf.at[pl.ds(start, rows), :], x_sem.at[i])

    def w_copies(col, size, slot):
        copies = []
        for i in range(n_pieces + 2):
            if i < 2:
                source = own_ref.at[i, :, pl.ds(col, size)]
                block = ids[1 + n_blocks] + i
            else:
                source = w_refs[i - 2].at[:, pl.ds(col, size)]
                block = ids[2 + n_blocks + i - 2]
            start = pl.multiple_of(block * half, half)
            copies.append(
                pltpu.make_async_copy(
                    source, w_buf.at[slot, pl.ds(start, half), pl.ds(0, size)], w_sem.at[slot, i]
                )
            )
        return copies

    full = cols // tile
    tail = cols - full * tile
    for i in range(n_blocks):
        x_copy(i).start()
    for copy in w_copies(0, tile, 0):
        copy.start()
    for i in range(n_blocks):
        x_copy(i).wait()
    row0 = lax.broadcasted_iota(jnp.int32, (time, 1), 0) == 0

    def product(slot, col, size):
        now = jnp.dot(x_buf[...], w_buf[slot, :width, :size], preferred_element_type=F32)
        prev = jnp.dot(x_buf[...], w_buf[slot, width:, :size], preferred_element_type=F32)
        prev = jnp.where(row0, 0.0, pltpu.roll(prev, 1, 0))
        gate_buf[:, pl.ds(col, size)] = now + prev + bias_ref[:, pl.ds(col, size)]

    @pl.loop(0, full)
    def _(n):
        slot = lax.rem(n, 2)

        @pl.when(n + 1 < full)
        def _():
            for copy in w_copies(pl.multiple_of((n + 1) * tile, tile), tile, 1 - slot):
                copy.start()

        if tail:

            @pl.when(n + 1 == full)
            def _():
                for copy in w_copies(full * tile, tail, 1 - slot):
                    copy.start()

        for copy in w_copies(pl.multiple_of(n * tile, tile), tile, slot):
            copy.wait()
        product(slot, pl.multiple_of(n * tile, tile), tile)

    if tail:
        for copy in w_copies(full * tile, tail, full % 2):
            copy.wait()
        product(full % 2, full * tile, tail)

    scan(time, group, gate_buf, keep_ref, cot_ref, cell_buf, adj_buf, hid_ref, dg_ref, db_ref)


STEP = 16


def scan(time, group, gate_buf, keep_ref, cot_ref, cell_buf, adj_buf, hid_ref, dg_ref, db_ref):
    steps = time // STEP
    sub = lax.broadcasted_iota(jnp.int32, (8, LANES), 0)
    zeros = jnp.zeros((8, LANES), F32)

    def down(a, d):
        return pltpu.roll(a, d, 0)

    def up(a, d):
        return pltpu.roll(a, 8 - d, 0)

    def spread(a, r):
        return jnp.broadcast_to(a[r : r + 1, :], (8, LANES))

    @pl.loop(0, group // LANES)
    def _(block):
        lane = pl.multiple_of(block * LANES, LANES)
        z_at = pl.ds(lane, LANES)
        f_at = pl.ds(pl.multiple_of(group + lane, LANES), LANES)
        o_at = pl.ds(pl.multiple_of(2 * group + lane, LANES), LANES)

        def forward(i, carry):
            at = pl.multiple_of(i * STEP, STEP)
            outs = []
            for h in range(STEP // 8):
                here = pl.ds(at + 8 * h, 8)
                cand = jnp.tanh(gate_buf[here, z_at])
                forget = sigmoid(gate_buf[here, f_at])
                outgate = sigmoid(gate_buf[here, o_at])
                a = forget * keep_ref[here, :]
                b = (1.0 - forget) * cand
                gate_buf[here, z_at] = cand
                gate_buf[here, f_at] = forget
                gate_buf[here, o_at] = outgate
                for d in (1, 2, 4):
                    inside = sub >= d
                    b = b + a * jnp.where(inside, down(b, d), 0.0)
                    a = a * jnp.where(inside, down(a, d), 1.0)
                cell = b + a * carry
                carry = spread(b, 7) + spread(a, 7) * carry
                cell_buf[here, :] = cell
                outs.append(outgate * cell)
            hid_ref[pl.ds(at, STEP), z_at] = jnp.concatenate(outs, axis=0).astype(BF)
            return carry

        lax.fori_loop(0, steps, forward, zeros, unroll=4)

        def backward(n, state):
            adj_in, decay_in, later, total = state
            i = steps - 1 - n
            at = pl.multiple_of(i * STEP, STEP)
            grads = cot_ref[pl.ds(at, STEP), z_at].astype(F32)
            parts = []
            for h in reversed(range(STEP // 8)):
                here = pl.ds(at + 8 * h, 8)
                cand = gate_buf[here, z_at]
                forget = gate_buf[here, f_at]
                outgate = gate_buf[here, o_at]
                keep = keep_ref[here, :]
                cell = cell_buf[here, :]
                first = at + 8 * h == 0
                before = cell_buf[pl.ds(jnp.maximum(at + 8 * h - 8, 0), 8), :]
                before = jnp.where(first, 0.0, before)
                prev = jnp.where(sub == 0, down(before, 1), down(cell, 1))
                g = grads[8 * h : 8 * h + 8]
                decay = forget * keep
                a = jnp.where(sub == 7, decay_in, up(decay, 1))
                b = g * outgate
                for d in (1, 2, 4):
                    inside = sub < 8 - d
                    b = b + a * jnp.where(inside, up(b, d), 0.0)
                    a = a * jnp.where(inside, up(a, d), 1.0)
                adj = b + a * adj_in
                adj_in = spread(b, 0) + spread(a, 0) * adj_in
                decay_in = spread(decay, 0)
                omf = 1.0 - forget
                scaled = adj * omf
                d_z = scaled * (1.0 - cand * cand)
                d_f = scaled * forget * (keep * prev - cand)
                d_o = g * cell * (outgate * (1.0 - outgate))
                parts.append((d_z, d_f, d_o))
            parts.reverse()
            new_later, new_total = [], []
            for gate, where in enumerate((z_at, f_at, o_at)):
                tiles = [part[gate].astype(BF) for part in parts]
                wide = [t.astype(F32) for t in tiles]
                dg_ref[0, pl.ds(at, STEP), where] = jnp.concatenate(tiles, axis=0)
                follow = wide[1:] + [None]
                moved = []
                for t, nxt in zip(wide, follow):
                    edge = later[gate] if nxt is None else spread(nxt, 0)
                    moved.append(jnp.where(sub == 7, edge, up(t, 1)))
                dg_ref[1, pl.ds(at, STEP), where] = jnp.concatenate(moved, axis=0).astype(BF)
                new_later.append(spread(wide[0], 0))
                new_total.append(total[gate] + functools.reduce(jnp.add, wide))
            return adj_in, decay_in, tuple(new_later), tuple(new_total)

        triple = (zeros, zeros, zeros)
        _, _, _, total = lax.fori_loop(0, steps, backward, (zeros, zeros, triple, triple), unroll=2)
        for gate, where in enumerate((z_at, f_at, o_at)):
            db_ref[:, where] = total[gate]


def gates_call(ids, blocks, own, pieces, bias, keep, cot, group):
    rows = blocks[0].shape[1]
    width = blocks[0].shape[2]
    half = own.shape[1]
    cols = own.shape[2]
    time = keep.shape[0]
    tile = min(256, cols)
    flops = 2 * time * 2 * width * cols
    kernel = functools.partial(gates_kernel, rows, half, len(blocks), len(pieces), group)
    return pl.pallas_call(
        kernel,
        out_shape=(
            jax.ShapeDtypeStruct((time, group), BF),
            jax.ShapeDtypeStruct((2, time, cols), BF),
            jax.ShapeDtypeStruct((8, cols), F32),
        ),
        in_specs=[smem_spec()]
        + [any_spec()] * (len(blocks) + 1 + len(pieces))
        + [vmem_spec()] * 3,
        out_specs=(vmem_spec(),) * 3,
        scratch_shapes=[
            pltpu.VMEM((time, width), BF),
            pltpu.VMEM((2, 2 * width, tile), BF),
            pltpu.VMEM((time, cols), F32),
            pltpu.VMEM((time, LANES), F32),
            pltpu.VMEM((time, LANES), F32),
            pltpu.SemaphoreType.DMA((len(blocks),)),
            pltpu.SemaphoreType.DMA((2, len(pieces) + 2)),
        ],
        compiler_params=pltpu.CompilerParams(vmem_limit_bytes=VMEM_BYTES),
        cost_estimate=pl.CostEstimate(
            flops=flops, bytes_accessed=2 * width * cols * 2 + time * width * 2 + time * cols * 6, transcendentals=0
        ),
        name="gates",
    )(ids, *blocks, own, *pieces, bias, keep, cot)


def inputs_kernel(half, n_pieces, chunk, groups, ids, *refs):
    dg_refs = refs[:groups]
    weights = [refs[groups + g * (n_pieces + 1) : groups + (g + 1) * (n_pieces + 1)] for g in range(groups)]
    mine_ref, all_ref = refs[groups + groups * (n_pieces + 1) : groups + groups * (n_pieces + 1) + 2]
    w_buf, acc, w_sem = refs[groups + groups * (n_pieces + 1) + 2 :]
    time, width = acc.shape

    def w_copies(g, col, size, slot):
        copies = []
        for i in range(n_pieces + 2):
            if i < 2:
                source = weights[g][0].at[i, :, pl.ds(col, size)]
                block = ids[1] + i
            else:
                source = weights[g][i - 1].at[:, pl.ds(col, size)]
                block = ids[2 + i - 2]
            start = pl.multiple_of(block * half, half)
            copies.append(
                pltpu.make_async_copy(
                    source, w_buf.at[slot, pl.ds(start, half), pl.ds(0, size)], w_sem.at[slot, i]
                )
            )
        return copies

    jobs = []
    for g in range(groups):
        cols = dg_refs[g].shape[2]
        col = 0
        while col < cols:
            size = min(chunk, cols - col)
            jobs.append((g, col, size))
            col += size
    step = 256 if width % 256 == 0 else LANES
    for copy in w_copies(*jobs[0], 0):
        copy.start()
    for n, (g, col, size) in enumerate(jobs):
        slot = n % 2
        if n + 1 < len(jobs):
            for copy in w_copies(*jobs[n + 1], 1 - slot):
                copy.start()
        for copy in w_copies(g, col, size, slot):
            copy.wait()

        @pl.loop(0, width // step)
        def _(k):
            at = pl.ds(pl.multiple_of(k * step, step), step)
            total = None if n == 0 else acc[:, at]
            for tap in range(2):
                rows = pl.ds(pl.multiple_of(tap * width + k * step, LANES), step)
                part = lax.dot_general(
                    dg_refs[g][tap, :, col : col + size],
                    w_buf[slot, rows, :size],
                    (((1,), (1,)), ((), ())),
                    preferred_element_type=F32,
                )
                total = part if total is None else total + part
            acc[:, at] = total

    own = mine_ref.shape[0]
    mine_ref[...] = acc[pl.ds(pl.multiple_of(ids[0] * own, own), own), :]
    all_ref[...] = acc[...].astype(BF)


def inputs_call(ids, dgs, weights, own_rows, width):
    groups = len(dgs)
    n_pieces = len(weights[0]) - 1
    half = weights[0][0].shape[1]
    time = dgs[0].shape[1]
    cols = sum(d.shape[2] for d in dgs)
    chunk = 512
    kernel = functools.partial(inputs_kernel, half, n_pieces, chunk, groups)
    flat = [w for group in weights for w in group]
    return pl.pallas_call(
        kernel,
        out_shape=(
            jax.ShapeDtypeStruct((own_rows, width), F32),
            jax.ShapeDtypeStruct((time, width), BF),
        ),
        in_specs=[smem_spec()] + [vmem_spec()] * groups + [any_spec()] * len(flat),
        out_specs=(vmem_spec(),) * 2,
        scratch_shapes=[
            pltpu.VMEM((2, 2 * width, chunk), BF),
            pltpu.VMEM((time, width), F32),
            pltpu.SemaphoreType.DMA((2, n_pieces + 2)),
        ],
        compiler_params=pltpu.CompilerParams(vmem_limit_bytes=VMEM_BYTES),
        cost_estimate=pl.CostEstimate(
            flops=2 * time * 2 * width * cols,
            bytes_accessed=2 * width * cols * 2 + time * cols * 4 + time * width * 4,
            transcendentals=0,
        ),
        name="grad_in",
    )(ids, *dgs, *flat)


def ring_kernel(n_received, ids, x_ref, mine_ref, other_ref, *refs):
    out_ref = refs[-1]
    total = jnp.dot(x_ref[0, 0], mine_ref[0], preferred_element_type=F32)
    total = total + jnp.dot(x_ref[1, 0], other_ref[0], preferred_element_type=F32)
    for ref in refs[:n_received]:
        total = total + ref[...].astype(F32)
    out_ref[...] = total.astype(out_ref.dtype)


def ring_call(ids, x_t, mine, other, received, tile, dtype):
    half, time = x_t.shape[2:]
    cols = mine.shape[2]
    flat = pl.BlockSpec((half, tile), lambda n, ids: (0, n))
    return pl.pallas_call(
        functools.partial(ring_kernel, len(received)),
        out_shape=jax.ShapeDtypeStruct((half, cols), dtype),
        grid_spec=pltpu.PrefetchScalarGridSpec(
            num_scalar_prefetch=1,
            grid=(cols // tile,),
            in_specs=[
                pl.BlockSpec((2, 1, half, time), lambda n, ids: (0, ids[0], 0, 0)),
                pl.BlockSpec((1, time, tile), lambda n, ids: (ids[1], 0, n)),
                pl.BlockSpec((1, time, tile), lambda n, ids: (ids[1], 0, n)),
            ]
            + [flat] * len(received),
            out_specs=flat,
        ),
        compiler_params=pltpu.CompilerParams(vmem_limit_bytes=VMEM_BYTES),
        cost_estimate=pl.CostEstimate(
            flops=4 * half * time * cols, bytes_accessed=4 * time * cols + 8 * half * cols, transcendentals=0
        ),
        name="grad_w",
    )(ids, x_t, mine, other, *received)


def shards(inputs, weight, bias, reset, cotangent):
    batches, _, rows, width = inputs.shape
    shard_rows, gate_cols = weight.shape
    n_stream = lax.axis_size("stream")
    n_stretch = lax.axis_size("stretch")
    n_x = n_stretch // 2
    time = rows * n_stretch
    half = shard_rows // 2
    per_tap = n_stream // 2
    feats = width // n_x
    s = lax.axis_index("stretch")
    p = lax.axis_index("stream")
    x, c = s // 2, lax.rem(s, 2)
    sign = 1 - 2 * c

    order = ring_order(n_stream)
    place_of = [order.index(i) for i in range(n_stream)]
    r = jnp.array(place_of, jnp.int32)[p]
    order_arr = jnp.array(order, jnp.int32)

    def owner(steps):
        return order_arr[lax.rem(r + sign * steps + n_stream, n_stream)]

    def ring_pairs(forward):
        pairs = []
        for st in range(n_stretch):
            up = (st % 2 == 0) == forward
            for i in range(n_stream):
                j = (place_of[i] + (1 if up else -1)) % n_stream
                pairs.append((st * n_stream + i, st * n_stream + order[j]))
        return pairs

    long_pairs, short_pairs = ring_pairs(True), ring_pairs(False)
    hops = n_stream // 2

    def ring(a, pairs):
        return lax.ppermute(a, ("stretch", "stream"), pairs)

    def to_core(a):
        return lax.ppermute(a, "stretch", [(i, i ^ 1) for i in range(n_stretch)])

    def to_x(a, k):
        return lax.ppermute(a, "stretch", [(i, i ^ (2 * k)) for i in range(n_stretch)])

    def by_x(options):
        out = options[0]
        for i in range(1, n_x):
            out = jnp.where(x == i, options[i], out)
        return out

    def by_core(first, second):
        return jnp.where(c == 0, first, second), jnp.where(c == 0, second, first)

    tiles = -(-feats // LANES)
    first = tiles // 2
    sizes = [first * LANES, (tiles - first) * LANES]
    starts = [0, first * LANES]

    def columns(a, start, size, gates=3):
        real = min(size, feats - start)
        options = []
        for i in range(n_x):
            parts = []
            for gate in range(gates):
                at = gate * width + i * feats + start
                part = a[..., at : at + real]
                if real < size:
                    part = jnp.pad(part, [(0, 0)] * (a.ndim - 1) + [(0, size - real)])
                parts.append(part)
            options.append(jnp.concatenate(parts, axis=-1) if gates > 1 else parts[0])
        return by_x(options)

    tokens = inputs.reshape(batches, rows, width)
    cots = cotangent.reshape(batches, rows, width)
    own_weights = [
        columns(weight, start, size).reshape(2, half, 3 * size) for start, size in zip(starts, sizes)
    ]
    from_x = [tokens] + [to_x(tokens, k) for k in range(1, n_x)]
    blocks = from_x + [to_core(b) for b in from_x]
    places = [(x ^ k) * 2 + c for k in range(n_x)] + [(x ^ k) * 2 + (1 - c) for k in range(n_x)]

    pieces, at_block = [], []
    for g, own in enumerate(own_weights):
        mine = lax.dynamic_index_in_dim(own, c, 0, False)
        forth = back = mine
        got = []
        for t in range(1, hops + 1):
            forth = ring(forth, long_pairs)
            got.append((forth, owner(-t), owner(t)))
            if t < hops:
                back = ring(back, short_pairs)
                got.append((back, owner(t), owner(-t)))
        group = []
        for piece, source, other in got:
            group += [piece, to_core(piece)]
            if g == 0:
                at_block += [2 * source + c, 2 * other + (1 - c)]
        pieces.append(group)

    cot_mine = lax.dynamic_index_in_dim(cots, c, 0, False)
    cot_other = to_core(lax.dynamic_index_in_dim(cots, 1 - c, 0, False))
    cot_pair = jnp.concatenate(by_core(cot_mine, cot_other), axis=0)
    cot_parts = [cot_pair[:, i * feats : (i + 1) * feats] for i in range(n_x)]
    cot_by_k = [by_x(cot_parts)]
    for k in range(1, n_x):
        cot_by_k.append(to_x(by_x([cot_parts[i ^ k] for i in range(n_x)]), k))
    cot_all = jnp.concatenate([by_x([cot_by_k[i ^ j] for j in range(n_x)]) for i in range(n_x)], axis=0)

    resets = lax.all_gather(reset.reshape(batches, rows).astype(F32), "stretch")
    keep = 1.0 - lax.dynamic_index_in_dim(resets, c, 1, False).reshape(time, 1)

    block_ids = jnp.stack([c] + places + [2 * p] + at_block).astype(jnp.int32)
    hiddens, dgs, biases = [], [], []
    for g, (start, size) in enumerate(zip(starts, sizes)):
        bias_g = columns(bias[None, :], start, size)
        real = min(size, feats - start)
        cot_g = cot_all[:, start : start + real]
        if real < size:
            cot_g = jnp.pad(cot_g, [(0, 0), (0, size - real)])
        hid, dg, db = gates_call(block_ids, blocks, own_weights[g], pieces[g], bias_g, keep, cot_g, size)
        hiddens.append(hid[:, :real])
        dgs.append(dg)
        biases.append(jnp.sum(db, axis=0).reshape(3, size)[:, :real])
    others = [to_core(dg) for dg in dgs]

    every = [None] * n_stretch
    whole = jnp.zeros((batches, time, width), BF)
    for block, place in zip(blocks, places):
        whole = lax.dynamic_update_slice(whole, block, (0, place * rows, 0))
    x_t = whole.transpose(0, 2, 1).reshape(batches, per_tap, 2, half, time)
    x_t = lax.dynamic_index_in_dim(x_t, c, 2, False)
    x_t = jnp.stack(by_core(x_t[0], x_t[1]))

    def ids_of(shard):
        return jnp.stack([lax.rem(shard, per_tap), shard // per_tap]).astype(jnp.int32)

    sums = []
    for dg, other, size in zip(dgs, others, sizes):
        forth, back = [], []
        for t in range(hops):
            forth = [ring(ring_call(ids_of(owner(hops - t)), x_t, dg, other, forth, size, BF), long_pairs)]
            if t < hops - 1:
                shard = owner(-(hops - 1 - t))
                back = [ring(ring_call(ids_of(shard), x_t, dg, other, back, size, BF), short_pairs)]
        sums.append(ring_call(ids_of(p), x_t, dg, other, forth + back, size, F32))

    in_ids = jnp.stack([x, 2 * p] + at_block).astype(jnp.int32)
    own_rows = time // n_x
    d_mine, d_all = inputs_call(
        in_ids, dgs, [[own_weights[g]] + pieces[g] for g in range(2)], own_rows, width
    )
    d_all = d_all.reshape(n_x, own_rows, width)
    for k in range(1, n_x):
        d_mine = d_mine + to_x(lax.dynamic_index_in_dim(d_all, x ^ k, 0, False), k).astype(F32)
    d_mine = d_mine.reshape(2, rows, width)
    keep_part = lax.dynamic_index_in_dim(d_mine, c, 0, False)
    send_part = to_core(lax.dynamic_index_in_dim(d_mine, 1 - c, 0, False))
    grad_inputs = jnp.stack(by_core(keep_part, send_part)).reshape(inputs.shape)

    hid = jnp.concatenate(hiddens, axis=1).reshape(n_x, own_rows, feats)
    hid_by_k = [lax.dynamic_index_in_dim(hid, x, 0, False)]
    for k in range(1, n_x):
        hid_by_k.append(to_x(lax.dynamic_index_in_dim(hid, x ^ k, 0, False), k))
    hid = jnp.concatenate([by_x([hid_by_k[i ^ j] for j in range(n_x)]) for i in range(n_x)], axis=1)
    hid = hid.reshape(2, rows, width)
    keep_part = lax.dynamic_index_in_dim(hid, c, 0, False)
    send_part = to_core(lax.dynamic_index_in_dim(hid, 1 - c, 0, False))
    hidden = jnp.stack(by_core(keep_part, send_part)).reshape(inputs.shape)

    parts = [[None] * n_x for _ in sizes]
    for g, (total, start, size) in enumerate(zip(sums, starts, sizes)):
        real = min(size, feats - start)
        got = [total] + [to_x(total, k) for k in range(1, n_x)]
        got = [jnp.concatenate(by_core(a, to_core(a)), axis=0) for a in got]
        for i in range(n_x):
            piece = by_x([got[i ^ j] for j in range(n_x)])
            parts[g][i] = piece.reshape(shard_rows, 3, size)[:, :, :real]
    pieces_out = []
    for gate in range(3):
        for i in range(n_x):
            for g in range(2):
                pieces_out.append(parts[g][i][:, gate])
    grad_weight = jnp.concatenate(pieces_out, axis=1)

    bias_part = jnp.concatenate(biases, axis=1)
    bias_part = lax.psum(bias_part, "stream")
    spread = jnp.zeros((3, n_x, feats), F32)
    spread = lax.dynamic_update_slice(spread, bias_part[:, None, :], (0, x, 0))
    grad_bias = lax.psum(spread.reshape(gate_cols), "stretch")
    return (hidden, grad_inputs, grad_weight, grad_bias)


def solution(mesh):
    in_specs = (
        P(None, "stream", "stretch", None),
        P("stream", None),
        P(),
        P(None, "stream", "stretch"),
        P(None, "stream", "stretch", None),
    )
    out_specs = (
        P(None, "stream", "stretch", None),
        P(None, "stream", "stretch", None),
        P("stream", None),
        P(),
    )
    return jax.shard_map(shards, mesh=mesh, in_specs=in_specs, out_specs=out_specs, check_vma=False)
```

```python
import functools

import jax
import jax.numpy as jnp
import numpy as np
from jax import lax
from jax.experimental import pallas as pl
from jax.experimental.pallas import tpu as pltpu
from jax.sharding import PartitionSpec as P

BF = jnp.bfloat16
F32 = jnp.float32
LANES = 128
VMEM_BYTES = 60 * 1024 * 1024


def cost(flops):
    return pl.CostEstimate(flops=int(1.6 * flops), bytes_accessed=10**6, transcendentals=0)


def any_spec():
    return pl.BlockSpec(memory_space=pl.ANY)


def vmem_spec():
    return pl.BlockSpec(memory_space=pltpu.VMEM)


def smem_spec():
    return pl.BlockSpec(memory_space=pltpu.SMEM)


def ring_order(count):
    inner = 1
    while (2 * inner) ** 2 <= count:
        inner *= 2
    outer = count // inner
    if inner == 1 or outer % 2:
        return list(range(count))
    order = [z * inner for z in range(outer)]
    for turn, z in enumerate(reversed(range(outer))):
        across = range(1, inner) if turn % 2 == 0 else reversed(range(1, inner))
        order += [z * inner + y for y in across]
    return order


def sigmoid(v):
    return 0.5 + 0.5 * jnp.tanh(0.5 * v)


def gates_kernel(at, rows, half, n_blocks, n_pieces, group, offset, ids, *refs):
    x_refs = refs[:n_blocks]
    own_ref = refs[n_blocks]
    w_refs = refs[n_blocks + 1 : n_blocks + 1 + n_pieces]
    bias_ref, keep_ref, cot_ref = refs[n_blocks + 1 + n_pieces : n_blocks + 4 + n_pieces]
    hid_ref, dg_ref, db_ref = refs[n_blocks + 4 + n_pieces : n_blocks + 7 + n_pieces]
    x_buf, w_buf, gate_buf, cell_buf, hid_buf, dg_buf, x_sem, w_sem, out_sem = refs[n_blocks + 7 + n_pieces :]
    time, width = x_buf.shape
    cols = gate_buf.shape[1]
    tile = w_buf.shape[2]
    batch = ids[at["core"]]

    def x_copy(i):
        start = pl.multiple_of(ids[at["time"] + i] * rows, rows)
        return pltpu.make_async_copy(x_refs[i].at[batch], x_buf.at[pl.ds(start, rows), :], x_sem.at[i])

    def w_copies(col, size, slot):
        copies = []
        for i in range(n_pieces + 2):
            if i < 2:
                source = own_ref.at[i, :, pl.ds(offset + col, size)]
                block = ids[at["pieces"]] + i
            else:
                source = w_refs[i - 2].at[:, pl.ds(offset + col, size)]
                block = ids[at["pieces"] + i - 1]
            start = pl.multiple_of(block * half, half)
            copies.append(
                pltpu.make_async_copy(
                    source, w_buf.at[slot, pl.ds(start, half), pl.ds(0, size)], w_sem.at[slot, i]
                )
            )
        return copies

    full = cols // tile
    tail = cols - full * tile
    for i in range(n_blocks):
        x_copy(i).start()
    for copy in w_copies(0, tile, 0):
        copy.start()
    for i in range(n_blocks):
        x_copy(i).wait()
    row0 = lax.broadcasted_iota(jnp.int32, (time, 1), 0) == 0

    def product(slot, col, size):
        now = jnp.dot(x_buf[...], w_buf[slot, :width, :size], preferred_element_type=F32)
        prev = jnp.dot(x_buf[...], w_buf[slot, width:, :size], preferred_element_type=F32)
        prev = jnp.where(row0, 0.0, pltpu.roll(prev, 1, 0))
        gate_buf[:, pl.ds(col, size)] = now + prev + bias_ref[:, pl.ds(col, size)]

    @pl.loop(0, full)
    def _(n):
        slot = lax.rem(n, 2)

        @pl.when(n + 1 < full)
        def _():
            for copy in w_copies(pl.multiple_of((n + 1) * tile, tile), tile, 1 - slot):
                copy.start()

        if tail:

            @pl.when(n + 1 == full)
            def _():
                for copy in w_copies(full * tile, tail, 1 - slot):
                    copy.start()

        for copy in w_copies(pl.multiple_of(n * tile, tile), tile, slot):
            copy.wait()
        product(slot, pl.multiple_of(n * tile, tile), tile)

    if tail:
        for copy in w_copies(full * tile, tail, full % 2):
            copy.wait()
        product(full % 2, full * tile, tail)

    def out_copies(block):
        lane = block * LANES
        if not isinstance(block, int):
            lane = pl.multiple_of(lane, LANES)
        copies = [pltpu.make_async_copy(hid_buf.at[block], hid_ref.at[:, pl.ds(lane, LANES)], out_sem.at[block, 0])]
        for gate in range(3):
            copies.append(
                pltpu.make_async_copy(
                    dg_buf.at[block, :, :, pl.ds(gate * LANES, LANES)],
                    dg_ref.at[:, :, pl.ds(gate * group + lane, LANES)],
                    out_sem.at[block, 1 + gate],
                )
            )
        return copies

    scan(time, group, gate_buf, keep_ref, cot_ref, cell_buf, hid_buf, dg_buf, db_ref, out_copies)
    for block in range(group // LANES):
        for copy in out_copies(block):
            copy.wait()


STEP = 16


def scan(time, group, gate_buf, keep_ref, cot_ref, cell_buf, hid_buf, dg_buf, db_ref, out_copies):
    steps = time // STEP
    sub = lax.broadcasted_iota(jnp.int32, (8, LANES), 0)
    zeros = jnp.zeros((8, LANES), F32)

    def down(a, d):
        return pltpu.roll(a, d, 0)

    def up(a, d):
        return pltpu.roll(a, 8 - d, 0)

    def spread(a, r):
        return jnp.broadcast_to(a[r : r + 1, :], (8, LANES))

    @pl.loop(0, group // LANES)
    def _(block):
        lane = pl.multiple_of(block * LANES, LANES)
        z_at = pl.ds(lane, LANES)
        f_at = pl.ds(pl.multiple_of(group + lane, LANES), LANES)
        o_at = pl.ds(pl.multiple_of(2 * group + lane, LANES), LANES)

        def forward(i, carry):
            at = pl.multiple_of(i * STEP, STEP)
            outs = []
            for h in range(STEP // 8):
                here = pl.ds(at + 8 * h, 8)
                cand = jnp.tanh(gate_buf[here, z_at])
                forget = sigmoid(gate_buf[here, f_at])
                outgate = sigmoid(gate_buf[here, o_at])
                a = forget * keep_ref[here, :]
                b = (1.0 - forget) * cand
                gate_buf[here, z_at] = cand
                gate_buf[here, f_at] = forget
                gate_buf[here, o_at] = outgate
                for d in (1, 2, 4):
                    inside = sub >= d
                    b = b + a * jnp.where(inside, down(b, d), 0.0)
                    a = a * jnp.where(inside, down(a, d), 1.0)
                cell = b + a * carry
                carry = spread(b, 7) + spread(a, 7) * carry
                cell_buf[here, :] = cell
                outs.append(outgate * cell)
            hid_buf[block, pl.ds(at, STEP), :] = jnp.concatenate(outs, axis=0).astype(BF)
            return carry

        lax.fori_loop(0, steps, forward, zeros, unroll=16)

        def backward(n, state):
            adj_in, decay_in, later, total = state
            i = steps - 1 - n
            at = pl.multiple_of(i * STEP, STEP)
            grads = cot_ref[pl.ds(at, STEP), z_at].astype(F32)
            parts = []
            for h in reversed(range(STEP // 8)):
                here = pl.ds(at + 8 * h, 8)
                cand = gate_buf[here, z_at]
                forget = gate_buf[here, f_at]
                outgate = gate_buf[here, o_at]
                keep = keep_ref[here, :]
                cell = cell_buf[here, :]
                first = at + 8 * h == 0
                before = cell_buf[pl.ds(jnp.maximum(at + 8 * h - 8, 0), 8), :]
                before = jnp.where(first, 0.0, before)
                prev = jnp.where(sub == 0, down(before, 1), down(cell, 1))
                g = grads[8 * h : 8 * h + 8]
                decay = forget * keep
                a = jnp.where(sub == 7, decay_in, up(decay, 1))
                b = g * outgate
                for d in (1, 2, 4):
                    inside = sub < 8 - d
                    b = b + a * jnp.where(inside, up(b, d), 0.0)
                    a = a * jnp.where(inside, up(a, d), 1.0)
                adj = b + a * adj_in
                adj_in = spread(b, 0) + spread(a, 0) * adj_in
                decay_in = spread(decay, 0)
                omf = 1.0 - forget
                scaled = adj * omf
                d_z = scaled * (1.0 - cand * cand)
                d_f = scaled * forget * (keep * prev - cand)
                d_o = g * cell * (outgate * (1.0 - outgate))
                parts.append((d_z, d_f, d_o))
            parts.reverse()
            new_later, new_total = [], []
            for gate, where in enumerate((z_at, f_at, o_at)):
                tiles = [part[gate].astype(BF) for part in parts]
                wide = [t.astype(F32) for t in tiles]
                dg_buf[block, 0, pl.ds(at, STEP), gate * LANES : (gate + 1) * LANES] = jnp.concatenate(tiles, axis=0)
                follow = wide[1:] + [None]
                moved = []
                for t, nxt in zip(wide, follow):
                    edge = later[gate] if nxt is None else spread(nxt, 0)
                    moved.append(jnp.where(sub == 7, edge, up(t, 1)))
                dg_buf[block, 1, pl.ds(at, STEP), gate * LANES : (gate + 1) * LANES] = jnp.concatenate(moved, axis=0).astype(BF)
                new_later.append(spread(wide[0], 0))
                new_total.append(total[gate] + functools.reduce(jnp.add, wide))
            return adj_in, decay_in, tuple(new_later), tuple(new_total)

        triple = (zeros, zeros, zeros)
        _, _, _, total = lax.fori_loop(0, steps, backward, (zeros, zeros, triple, triple), unroll=8)
        for gate, where in enumerate((z_at, f_at, o_at)):
            db_ref[:, where] = total[gate]
        for copy in out_copies(block):
            copy.start()


def gates_call(at, ids, blocks, own, pieces, offset, bias, keep, cot, group):
    rows = blocks[0].shape[1]
    width = blocks[0].shape[2]
    half = own.shape[1]
    cols = 3 * group
    time = keep.shape[0]
    tile = min(256, cols)
    kernel = functools.partial(gates_kernel, at, rows, half, len(blocks), len(pieces), group, offset)
    return pl.pallas_call(
        kernel,
        out_shape=(
            jax.ShapeDtypeStruct((time, group), BF),
            jax.ShapeDtypeStruct((2, time, cols), BF),
            jax.ShapeDtypeStruct((8, cols), F32),
        ),
        in_specs=[smem_spec()]
        + [any_spec()] * (len(blocks) + 1 + len(pieces))
        + [vmem_spec()] * 3,
        out_specs=(any_spec(), any_spec(), vmem_spec()),
        scratch_shapes=[
            pltpu.VMEM((time, width), BF),
            pltpu.VMEM((2, 2 * width, tile), BF),
            pltpu.VMEM((time, cols), F32),
            pltpu.VMEM((time, LANES), F32),
            pltpu.VMEM((group // LANES, time, LANES), BF),
            pltpu.VMEM((group // LANES, 2, time, 3 * LANES), BF),
            pltpu.SemaphoreType.DMA((len(blocks),)),
            pltpu.SemaphoreType.DMA((2, len(pieces) + 2)),
            pltpu.SemaphoreType.DMA((group // LANES, 4)),
        ],
        compiler_params=pltpu.CompilerParams(vmem_limit_bytes=VMEM_BYTES),
        cost_estimate=cost(2 * time * 2 * width * cols * 1.5),
        name="gates",
    )(ids, *blocks, own, *pieces, bias, keep, cot)


def inputs_kernel(at_id, k, half, n_pieces, chunk, units, ids, *refs):
    dg_refs = refs[: len(units)]
    groups = 1 + max(g for g, _ in units)
    at = len(units) + groups * (n_pieces + 1)
    weights = [refs[len(units) + g * (n_pieces + 1) : len(units) + (g + 1) * (n_pieces + 1)] for g in range(groups)]
    out_ref = refs[at]
    w_buf, dg_buf, acc, w_sem, dg_sem = refs[at + 1 :]
    rows, width = acc.shape
    row = pl.multiple_of(ids[at_id["far"] + k] * rows, rows)

    def w_copies(g, col, size, slot):
        copies = []
        for i in range(n_pieces + 2):
            if i < 2:
                source = weights[g][0].at[i, :, pl.ds(col, size)]
                block = ids[at_id["pieces"]] + i
            else:
                source = weights[g][i - 1].at[:, pl.ds(col, size)]
                block = ids[at_id["pieces"] + i - 1]
            start = pl.multiple_of(block * half, half)
            copies.append(
                pltpu.make_async_copy(
                    source, w_buf.at[slot, pl.ds(start, half), pl.ds(0, size)], w_sem.at[slot, i]
                )
            )
        return copies

    firsts = [sum(ref.shape[2] for ref in dg_refs[:u]) for u in range(len(units))]

    def dg_copy(u):
        cols = dg_refs[u].shape[2]
        return pltpu.make_async_copy(
            dg_refs[u].at[:, pl.ds(row, rows), :], dg_buf.at[:, :, pl.ds(firsts[u], cols)], dg_sem.at[u]
        )

    jobs = []
    for u, (g, offset) in enumerate(units):
        cols = dg_refs[u].shape[2]
        for col in range(0, cols, chunk):
            jobs.append((u, col, (g, offset + col, min(chunk, cols - col))))
    step = 768 if width % 768 == 0 else LANES
    dg_copy(0).start()
    for copy in w_copies(*jobs[0][2], 0):
        copy.start()
    for u in range(1, len(units)):
        dg_copy(u).start()
    for n, (u, col, job) in enumerate(jobs):
        slot, size = n % 2, job[2]
        if n + 1 < len(jobs):
            for copy in w_copies(*jobs[n + 1][2], 1 - slot):
                copy.start()
        if col == 0:
            dg_copy(u).wait()
        for copy in w_copies(*job, slot):
            copy.wait()
        here = slice(firsts[u] + col, firsts[u] + col + size)

        @pl.loop(0, width // step)
        def _(k):
            at = pl.ds(pl.multiple_of(k * step, step), step)
            total = None if n == 0 else acc[:, at]
            for tap in range(2):
                feats = pl.ds(pl.multiple_of(tap * width + k * step, LANES), step)
                part = lax.dot_general(
                    dg_buf[tap, :, here],
                    w_buf[slot, feats, :size],
                    (((1,), (1,)), ((), ())),
                    preferred_element_type=F32,
                )
                total = part if total is None else total + part
            if n + 1 < len(jobs):
                acc[:, at] = total
            else:
                out_ref[:, at] = total.astype(out_ref.dtype)


def inputs_call(at, ids, k, dgs, weights, units, rows, width, dtype):
    n_pieces = len(weights[0]) - 1
    half = weights[0][0].shape[1]
    cols = sum(d.shape[2] for d in dgs)
    chunk = 768
    flat = [w for group in weights for w in group]
    return pl.pallas_call(
        functools.partial(inputs_kernel, at, k, half, n_pieces, chunk, units),
        out_shape=jax.ShapeDtypeStruct((rows, width), dtype),
        in_specs=[smem_spec()] + [any_spec()] * (len(dgs) + len(flat)),
        out_specs=vmem_spec(),
        scratch_shapes=[
            pltpu.VMEM((2, 2 * width, chunk), BF),
            pltpu.VMEM((2, rows, cols), BF),
            pltpu.VMEM((rows, width), F32),
            pltpu.SemaphoreType.DMA((2, n_pieces + 2)),
            pltpu.SemaphoreType.DMA((len(dgs),)),
        ],
        compiler_params=pltpu.CompilerParams(vmem_limit_bytes=VMEM_BYTES),
        cost_estimate=cost(2 * rows * 2 * width * cols),
        name="grad_in",
    )(ids, *dgs, *flat)


def turn_kernel(at, n_blocks, half, ids, *refs):
    x_refs, out_ref = refs[:n_blocks], refs[n_blocks]
    x_buf, t_buf, sem = refs[n_blocks + 1 :]
    rows = x_buf.shape[1]
    core = ids[at["core"]]
    jobs = [(i, m) for i in range(n_blocks) for m in range(2)]

    def load(n):
        i, m = jobs[n]
        batch = core if m == 0 else 1 - core
        return pltpu.make_async_copy(x_refs[i].at[batch], x_buf.at[n % 2], sem.at[n % 2])

    load(0).start()
    for n, (i, m) in enumerate(jobs):
        if n + 1 < len(jobs):
            load(n + 1).start()
        load(n).wait()
        t_buf[...] = x_buf[n % 2].T
        column = pl.ds(pl.multiple_of(ids[at["time"] + i] * rows, rows), rows)
        for q in range(out_ref.shape[1]):
            start = pl.multiple_of(q * 2 * half + core * half, 16)
            out_ref[m, q, :, column] = t_buf[pl.ds(start, half), :]


def turn_call(at, ids, blocks, per_tap, half, time):
    _, rows, width = blocks[0].shape
    return pl.pallas_call(
        functools.partial(turn_kernel, at, len(blocks), half),
        out_shape=jax.ShapeDtypeStruct((2, per_tap, half, time), BF),
        in_specs=[smem_spec()] + [any_spec()] * len(blocks),
        out_specs=vmem_spec(),
        scratch_shapes=[
            pltpu.VMEM((2, rows, width), BF),
            pltpu.VMEM((width, rows), BF),
            pltpu.SemaphoreType.DMA((2,)),
        ],
        compiler_params=pltpu.CompilerParams(vmem_limit_bytes=VMEM_BYTES),
        cost_estimate=cost(7 * 10**9),
        name="turn",
    )(ids, *blocks)


def weight_kernel(count, x_ref, *refs):
    mine_refs, other_refs, out_ref = refs[:count], refs[count : 2 * count], refs[2 * count]
    x_buf, dg_buf, out_buf, x_sem, in_sem, out_sem = refs[2 * count + 1 :]
    pieces, half, time = x_ref.shape[1:]
    jobs, col = [], 0
    for u in range(count):
        for tap in range(2):
            jobs.append((u, tap, col))
        col += mine_refs[u].shape[2]

    def x_copy(m):
        return pltpu.make_async_copy(x_ref.at[m], x_buf.at[m], x_sem.at[m])

    def dg_copies(n):
        u, tap, _ = jobs[n]
        size = mine_refs[u].shape[2]
        return [
            pltpu.make_async_copy(ref.at[tap], dg_buf.at[n % 2, m, :, pl.ds(0, size)], in_sem.at[n % 2, m])
            for m, ref in enumerate((mine_refs[u], other_refs[u]))
        ]

    def out_copy(n):
        u, tap, first = jobs[n]
        size = mine_refs[u].shape[2]
        return pltpu.make_async_copy(
            out_buf.at[n % 2, :, :, pl.ds(0, size)], out_ref.at[tap, :, :, pl.ds(first, size)], out_sem.at[n % 2]
        )

    x_copy(0).start()
    for copy in dg_copies(0):
        copy.start()
    x_copy(1).start()
    for n, (u, tap, first) in enumerate(jobs):
        size = mine_refs[u].shape[2]
        slot = n % 2
        if n + 1 < len(jobs):
            for copy in dg_copies(n + 1):
                copy.start()
        if n == 0:
            x_copy(0).wait()
            x_copy(1).wait()
        for copy in dg_copies(n):
            copy.wait()
        if n >= 2:
            out_copy(n - 2).wait()
        tile = 256 if size % 256 == 0 else LANES

        @pl.loop(0, size // tile)
        def _(k):
            at = pl.ds(pl.multiple_of(k * tile, tile), tile)
            total = None
            for m in range(2):
                part = jnp.dot(
                    x_buf[m].reshape(pieces * half, time), dg_buf[slot, m, :, at], preferred_element_type=F32
                )
                total = part if total is None else total + part
            out_buf[slot, :, :, at] = total.reshape(pieces, half, tile)

        out_copy(n).start()
    for n in range(max(0, len(jobs) - 2), len(jobs)):
        out_copy(n).wait()


def weight_call(x_t, mine, other):
    _, pieces, half, time = x_t.shape
    cols = sum(d.shape[2] for d in mine)
    most = max(d.shape[2] for d in mine)
    return pl.pallas_call(
        functools.partial(weight_kernel, len(mine)),
        out_shape=jax.ShapeDtypeStruct((2, pieces, half, cols), F32),
        in_specs=[any_spec()] * (1 + 2 * len(mine)),
        out_specs=any_spec(),
        scratch_shapes=[
            pltpu.VMEM(x_t.shape, BF),
            pltpu.VMEM((2, 2, time, most), BF),
            pltpu.VMEM((2, pieces, half, most), F32),
            pltpu.SemaphoreType.DMA((2,)),
            pltpu.SemaphoreType.DMA((2, 2)),
            pltpu.SemaphoreType.DMA((2,)),
        ],
        compiler_params=pltpu.CompilerParams(vmem_limit_bytes=VMEM_BYTES),
        cost_estimate=cost(8 * pieces * half * time * cols),
        name="grad_w",
    )(x_t, *mine, *other)


def place_kernel(at_id, count, spans, feats, width, ids, *refs):
    parts, out_ref = refs[:count], refs[-4]
    buf, in_sem, out_sem = refs[-3:]
    half = buf.shape[1]
    loads = [pltpu.make_async_copy(parts[i], buf.at[i], in_sem.at[i]) for i in range(count)]
    for copy in loads:
        copy.start()
    stores = []
    for i in range(count):
        loads[i].wait()
        row = pl.multiple_of(ids[at_id["place"] + 2 * i] * half, half)
        col = 0
        for start, size in spans:
            for gate in range(3):
                at = pl.multiple_of(gate * width + ids[at_id["place"] + 2 * i + 1] * feats + start, LANES)
                stores.append(
                    pltpu.make_async_copy(
                        buf.at[i, :, pl.ds(col, size)],
                        out_ref.at[pl.ds(row, half), pl.ds(at, size)],
                        out_sem.at[len(stores)],
                    )
                )
                stores[-1].start()
                col += size
    for copy in stores:
        copy.wait()


def place_call(at, ids, parts, out, spans, feats, rows, width):
    half, cols = parts[0].shape
    extra = [] if out is None else [out]
    return pl.pallas_call(
        functools.partial(place_kernel, at, len(parts), spans, feats, width),
        out_shape=jax.ShapeDtypeStruct((rows, 3 * width), F32),
        in_specs=[smem_spec()] + [any_spec()] * (len(parts) + len(extra)),
        out_specs=any_spec(),
        scratch_shapes=[
            pltpu.VMEM((len(parts), half, cols), F32),
            pltpu.SemaphoreType.DMA((len(parts),)),
            pltpu.SemaphoreType.DMA((3 * len(spans) * len(parts),)),
        ],
        input_output_aliases={1 + len(parts): 0} if extra else {},
        compiler_params=pltpu.CompilerParams(vmem_limit_bytes=VMEM_BYTES),
        cost_estimate=cost(5 * 10**9),
        name="place",
    )(ids, *parts, *extra)


def after(a, *others):
    return lax.optimization_barrier((a,) + others)[0] if others else a


class Links:
    def __init__(self):
        self.n_stream = lax.axis_size("stream")
        self.n_stretch = lax.axis_size("stretch")
        self.n_x = self.n_stretch // 2
        self.hops = self.n_stream // 2
        self.order = ring_order(self.n_stream)
        self.place_of = [self.order.index(i) for i in range(self.n_stream)]
        self.pairs = [self.ring_pairs(True), self.ring_pairs(False)]
        table = [self.numbers(s, p) for s in range(self.n_stretch) for p in range(self.n_stream)]
        self.at, total = {}, 0
        for name, numbers in table[0].items():
            self.at[name] = total
            total += len(numbers)
        flat = jnp.array(np.array([sum(row.values(), []) for row in table], np.int32))
        me = lax.axis_index("stretch") * self.n_stream + lax.axis_index("stream")
        self.ids = lax.dynamic_index_in_dim(flat, me, 0, False)
        self.x, self.c, self.p = (self.number(name) for name in ("x", "core", "stream"))

    def numbers(self, s, p):
        n, hops = self.n_stream, self.hops
        x, c, r = s // 2, s % 2, self.place_of[p]
        sign = 1 - 2 * c

        def owner(steps):
            return self.order[(r + sign * steps) % n]

        pieces = [2 * p]
        for t in range(1, hops + 1):
            pieces += [2 * owner(-t) + c, 2 * owner(t) + (1 - c)]
            if t < hops:
                pieces += [2 * owner(t) + c, 2 * owner(-t) + (1 - c)]
        far = [x ^ k for k in range(self.n_x)]
        return {
            "x": [x],
            "core": [c],
            "stream": [p],
            "time": [i * 2 + c for i in far] + [i * 2 + 1 - c for i in far],
            "pieces": pieces,
            "far": far,
            "place": [v for core in (c, 1 - c) for i in far for v in (core, i)],
            "forth": [owner(hops - t) for t in range(hops)],
            "back": [owner(t + 1 - hops) for t in range(hops - 1)],
        }

    def number(self, name, i=0):
        return self.ids[self.at[name] + i]

    def ring_pairs(self, forward):
        pairs = []
        for st in range(self.n_stretch):
            up = (st % 2 == 0) == forward
            for i in range(self.n_stream):
                j = (self.place_of[i] + (1 if up else -1)) % self.n_stream
                pairs.append((st * self.n_stream + i, st * self.n_stream + self.order[j]))
        return pairs

    def long(self, a):
        return lax.ppermute(a, ("stretch", "stream"), self.pairs[0])

    def short(self, a):
        return lax.ppermute(a, ("stretch", "stream"), self.pairs[1])

    def to_core(self, a):
        return lax.ppermute(a, "stretch", [(i, i ^ 1) for i in range(self.n_stretch)])

    def to_x(self, a, k):
        return lax.ppermute(a, "stretch", [(i, i ^ (2 * k)) for i in range(self.n_stretch)])

    def by_x(self, options):
        out = options[0]
        for i in range(1, self.n_x):
            out = jnp.where(self.x == i, options[i], out)
        return out

    def in_x_order(self, by_k):
        return [self.by_x([by_k[i ^ j] for j in range(self.n_x)]) for i in range(self.n_x)]

    def by_core(self, mine, other):
        return jnp.where(self.c == 0, mine, other), jnp.where(self.c == 0, other, mine)


class Gather:
    def __init__(self, links, mine):
        self.links = links
        self.forth = self.back = mine
        self.step = 0
        self.waiting, self.crossed, self.group, self.marks = [], [], [], []

    def cross(self):
        self.crossed = []
        for piece in self.waiting:
            self.crossed.append(self.links.to_core(piece))
            self.group += [piece, self.crossed[-1]]
        self.waiting = []

    def hop(self, *deps):
        links = self.links
        deps = tuple(self.crossed) + deps
        self.step += 1
        forth = links.long(after(self.forth, *deps))
        arriving = [forth]
        if self.step < links.hops:
            self.back = links.short(after(self.back, *deps))
            arriving.append(self.back)
            self.marks = arriving
        self.forth = forth
        self.cross()
        self.waiting = arriving

    def hops_until(self, last, *deps):
        while self.step < last:
            self.hop(*deps)
            deps = ()


class Reduce:
    def __init__(self, links, local):
        self.links, self.local = links, local
        self.forth = self.back = None
        self.step = 0

    def part(self, shard, incoming, deps):
        part = lax.dynamic_index_in_dim(self.local, shard, 0, False)
        part = part if incoming is None else part + incoming.astype(F32)
        return after(part.astype(BF), *deps)

    def hop(self, *deps):
        links, t = self.links, self.step
        self.step += 1
        sent = [self.part(links.number("forth", t), self.forth, deps)]
        self.forth = links.long(sent[0])
        if t < links.hops - 1:
            sent.append(self.part(links.number("back", t), self.back, deps))
            self.back = links.short(sent[1])
        return sent

    def hops_until(self, last, *deps):
        sent = []
        while self.step < last:
            sent = self.hop(*deps)
            deps = ()
        return sent

    def total(self, *deps):
        own = lax.dynamic_index_in_dim(self.local, self.links.p, 0, False)
        return own + after(self.forth, *deps).astype(F32) + self.back.astype(F32)


def shards(inputs, weight, bias, reset, cotangent):
    batches, _, rows, width = inputs.shape
    shard_rows, gate_cols = weight.shape
    links = Links()
    n_x, hops, x, c = links.n_x, links.hops, links.x, links.c
    at, ids = links.at, links.ids
    others_x = range(1, n_x)
    time = rows * links.n_stretch
    half = shard_rows // 2
    per_tap = links.n_stream // 2
    feats = width // n_x
    own_rows = time // n_x

    tiles = -(-feats // LANES)
    counts = [tiles // 5 + (1 if u in (0, 1, 3, 4)[: tiles % 5] else 0) for u in range(5)]
    sizes = [count * LANES for count in counts]
    starts = [sum(sizes[:u]) for u in range(5)]
    reals = [min(size, feats - start) for start, size in zip(starts, sizes)]
    members = [[0], [1, 2], [3, 4]]
    place_in_group = [(0, 0), (1, 0), (1, 3 * sizes[1]), (2, 0), (2, 3 * sizes[3])]
    grad_members = [[0, 1, 2], [3, 4]]

    def columns(a, u):
        options = []
        for i in range(n_x):
            parts = []
            for gate in range(3):
                first_col = gate * width + i * feats + starts[u]
                part = a[..., first_col : first_col + reals[u]]
                if reals[u] < sizes[u]:
                    part = jnp.pad(part, [(0, 0)] * (a.ndim - 1) + [(0, sizes[u] - reals[u])])
                parts.append(part)
            options.append(jnp.concatenate(parts, axis=-1))
        return links.by_x(options)

    def halves(g):
        parts = [columns(weight, u) for u in members[g]]
        return jnp.concatenate(parts, axis=1).reshape(2, half, -1)

    def mine_of(own, *deps):
        return after(lax.dynamic_index_in_dim(own, c, 0, False), *deps)

    tokens = inputs.reshape(batches, rows, width)
    cots = cotangent.reshape(batches, rows, width)
    mid = batches // 2

    own_weights = [halves(0)]
    first = Gather(links, mine_of(own_weights[0]))
    first.hop()
    core_tokens = links.to_core(tokens)
    x_first = [links.to_x(tokens[:mid], k) for k in others_x]
    cot_mine = lax.dynamic_index_in_dim(cots, c, 0, False)
    cot_other = links.to_core(lax.dynamic_index_in_dim(cots, 1 - c, 0, False))
    reset_mine = reset.reshape(batches, rows).astype(F32)
    reset_pair = jnp.stack(links.by_core(reset_mine, links.to_core(reset_mine)), axis=1)
    own_weights += [halves(1), halves(2)]
    first.hop(core_tokens, cot_other, reset_pair)
    first.hops_until(hops - 1)
    first.hop(*x_first)
    second = Gather(links, mine_of(own_weights[1], *first.marks))
    x_second = [links.to_x(after(tokens[mid:], *x_first), k) for k in others_x]

    cot_pair = jnp.concatenate(links.by_core(cot_mine, cot_other), axis=0)

    def cot_unit(u, *deps):
        parts = []
        for i in range(n_x):
            first_col = i * feats + starts[u]
            part = cot_pair[:, first_col : first_col + reals[u]]
            if reals[u] < sizes[u]:
                part = jnp.pad(part, [(0, 0), (0, sizes[u] - reals[u])])
            parts.append(part)
        by_k = [links.by_x(parts)]
        for k in others_x:
            leaving = links.by_x([parts[i ^ k] for i in range(n_x)])
            by_k.append(links.to_x(after(leaving, *deps), k))
        return jnp.concatenate(links.in_x_order(by_k), axis=0), by_k[1:]

    cot_units, cot_marks = [None] * 5, [None] * 5
    cot_units[0], cot_marks[0] = cot_unit(0, *x_first)
    reset_parts = [reset_pair] + [links.to_x(after(reset_pair, *x_first), k) for k in others_x]
    keep = jnp.stack(links.in_x_order(reset_parts), axis=1)
    keep = 1.0 - lax.dynamic_index_in_dim(keep, c, 0, False).reshape(time, 1)
    second.hop()
    first.cross()
    core_first = [links.to_core(a) for a in x_first]
    second.hop(*first.crossed, *core_first)
    second.hops_until(hops - 1, *x_second, *cot_marks[0], *reset_parts[1:])
    core_second = [links.to_core(a) for a in x_second]
    from_x = [jnp.concatenate(pair, axis=0) for pair in zip(x_first, x_second)]
    from_both = [jnp.concatenate(pair, axis=0) for pair in zip(core_first, core_second)]
    blocks = [tokens] + from_x + [core_tokens] + from_both
    for u in range(1, 5):
        cot_units[u], cot_marks[u] = cot_unit(u, *x_second)

    hiddens, dgs, others, biases = [], [], [], []

    def gates(u, gather, *deps):
        g, offset = place_in_group[u]
        bias_u = after(columns(bias[None, :], u), *deps)
        hid, dg, db = gates_call(
            at, ids, blocks, own_weights[g], gather.group, offset, bias_u, keep, cot_units[u], sizes[u]
        )
        hiddens.append(hid[:, : reals[u]])
        dgs.append(dg)
        others.append(links.to_core(dg))
        biases.append(jnp.sum(db, axis=0).reshape(3, sizes[u])[:, : reals[u]])
        return db

    def local_gradient(units):
        local = weight_call(x_t, [dgs[u] for u in units], [others[u] for u in units])
        return local.reshape(links.n_stream, half, -1)

    done = gates(0, first)
    second.hop(done)
    third = Gather(links, mine_of(own_weights[2], done, *second.marks))
    third.hop(*cot_marks[1], *cot_marks[2])
    second.cross()

    if half % 16 == 0 and rows % LANES == 0:
        x_t = turn_call(at, ids, blocks, per_tap, half, time)
    else:
        whole = jnp.zeros((batches, time, width), BF)
        for i, block in enumerate(blocks):
            whole = lax.dynamic_update_slice(whole, block, (0, links.number("time", i) * rows, 0))
        x_t = whole.transpose(0, 2, 1).reshape(batches, per_tap, 2, half, time)
        x_t = lax.dynamic_index_in_dim(x_t, c, 2, False)
        x_t = jnp.stack(links.by_core(x_t[0], x_t[1]))

    third.hop(x_t, *second.crossed)
    done = gates(1, second)
    third.hops_until(hops - 1, done, *cot_marks[3], *cot_marks[4])
    done = gates(2, second)
    third.hop(done)
    third.cross()

    red_first = Reduce(links, local_gradient(grad_members[0]))
    sent = red_first.hop()
    done = gates(3, third, *sent)
    sent = red_first.hop(done)
    done = gates(4, third, *sent)
    sent = red_first.hops_until(hops - 1, done)

    hid = jnp.concatenate(hiddens, axis=1).reshape(n_x, own_rows, feats)
    hid_by_k = [lax.dynamic_index_in_dim(hid, x, 0, False)]
    for k in others_x:
        hid_by_k.append(links.to_x(lax.dynamic_index_in_dim(hid, links.number("far", k), 0, False), k))
    hid = jnp.concatenate(links.in_x_order(hid_by_k), axis=1).reshape(2, rows, width)
    hid_mine = lax.dynamic_index_in_dim(hid, c, 0, False)
    hid_other = links.to_core(lax.dynamic_index_in_dim(hid, 1 - c, 0, False))
    hidden = jnp.stack(links.by_core(hid_mine, hid_other)).reshape(inputs.shape)

    pieces = [[own] + gather.group for own, gather in zip(own_weights, (first, second, third))]

    def d_inputs(k, dtype, *deps):
        now = [after(dgs[0], *deps)] + dgs[1:]
        return inputs_call(at, ids, k, now, pieces, place_in_group, own_rows, width, dtype)

    red_last = Reduce(links, local_gradient(grad_members[1]))
    sent = red_first.hop(red_last.local[0, 0, :1], *hid_by_k[1:])
    sent = red_last.hop(*sent)
    d_others = [d_inputs(k, BF, *sent) for k in others_x]
    d_received = [links.to_x(a, k) for a, k in zip(d_others, others_x)]

    bias_part = jnp.concatenate(biases, axis=1)
    bit = 1
    while bit < links.n_stream:
        swaps = [(i, i ^ bit) for i in range(links.n_stream)]
        bias_part = bias_part + lax.ppermute(bias_part, "stream", swaps)
        bit *= 2
    bias_part = bias_part + links.to_core(bias_part)
    bias_parts = [bias_part] + [links.to_x(bias_part, k) for k in others_x]
    grad_bias = jnp.stack(links.in_x_order(bias_parts), axis=1).reshape(gate_cols)

    aligned = feats % LANES == 0
    parts = [[None] * n_x for _ in sizes]

    def spread(total):
        scale = jnp.maximum(jnp.max(jnp.abs(total), axis=0, keepdims=True), 1e-30) * 2.0**-15
        coded, scale = lax.optimization_barrier(((total / scale).astype(jnp.float16), scale))
        scale = jnp.broadcast_to(scale, (8, scale.shape[1]))
        got = [(coded, scale)] + [(links.to_x(coded, k), links.to_x(scale, k)) for k in others_x]
        values = [a.astype(F32) * b[:1] for a, b in got]
        return values, [links.to_core(a) for a in values]

    def put(grad_weight, units, got, crossed):
        spans = [(starts[u], sizes[u]) for u in units]
        if aligned:
            return place_call(at, ids, got + crossed, grad_weight, spans, feats, shard_rows, width)
        got = [jnp.concatenate(links.by_core(a, b), axis=0) for a, b in zip(got, crossed)]
        col = 0
        ordered = links.in_x_order(got)
        for u in units:
            for i in range(n_x):
                piece = ordered[i][:, col : col + 3 * sizes[u]]
                parts[u][i] = piece.reshape(shard_rows, 3, sizes[u])[:, :, : reals[u]]
            col += 3 * sizes[u]
        return None

    got, crossed = spread(red_first.total(*d_others))
    sent = red_last.hop(*d_others)
    d_mine = d_inputs(0, F32, *sent)
    red_last.hops_until(hops - 1, d_mine, grad_bias, hidden, *got[1:])
    red_last.hop()
    grad_weight = put(None, grad_members[0], got, crossed)
    got, crossed = spread(red_last.total(*d_received))
    for a in d_received:
        d_mine = d_mine + a.astype(F32)
    d_mine = d_mine.reshape(2, rows, width)
    d_keep = lax.dynamic_index_in_dim(d_mine, c, 0, False)
    d_other = links.to_core(lax.dynamic_index_in_dim(d_mine, 1 - c, 0, False))
    grad_inputs = jnp.stack(links.by_core(d_keep, d_other)).reshape(inputs.shape)
    grad_weight = put(grad_weight, grad_members[1], got, crossed)
    if not aligned:
        grad_weight = jnp.concatenate(
            [parts[u][i][:, gate] for gate in range(3) for i in range(n_x) for u in range(5)], axis=1
        )
    return (hidden, grad_inputs, grad_weight, grad_bias)


def solution(mesh):
    in_specs = (
        P(None, "stream", "stretch", None),
        P("stream", None),
        P(),
        P(None, "stream", "stretch"),
        P(None, "stream", "stretch", None),
    )
    out_specs = (
        P(None, "stream", "stretch", None),
        P(None, "stream", "stretch", None),
        P("stream", None),
        P(),
    )
    return jax.shard_map(shards, mesh=mesh, in_specs=in_specs, out_specs=out_specs, check_vma=False)
```

```python
import functools

import jax
import jax.numpy as jnp
import numpy as np
from jax import lax
from jax.experimental import pallas as pl
from jax.experimental.pallas import tpu as pltpu
from jax.sharding import PartitionSpec as P

BF = jnp.bfloat16
F32 = jnp.float32
LANES = 128
VMEM_BYTES = 60 * 1024 * 1024


def cost(flops):
    return pl.CostEstimate(flops=int(5 * flops), bytes_accessed=10**6, transcendentals=0)


def any_spec():
    return pl.BlockSpec(memory_space=pl.ANY)


def vmem_spec():
    return pl.BlockSpec(memory_space=pltpu.VMEM)


def smem_spec():
    return pl.BlockSpec(memory_space=pltpu.SMEM)


def ring_order(count):
    inner = 1
    while (2 * inner) ** 2 <= count:
        inner *= 2
    outer = count // inner
    if inner == 1 or outer % 2:
        return list(range(count))
    order = [z * inner for z in range(outer)]
    for turn, z in enumerate(reversed(range(outer))):
        across = range(1, inner) if turn % 2 == 0 else reversed(range(1, inner))
        order += [z * inner + y for y in across]
    return order


def sigmoid(v):
    return 0.5 + 0.5 * jnp.tanh(0.5 * v)


def gates_kernel(at, rows, half, n_blocks, n_pieces, group, offset, ids, *refs):
    x_refs = refs[:n_blocks]
    own_ref = refs[n_blocks]
    w_refs = refs[n_blocks + 1 : n_blocks + 1 + n_pieces]
    bias_ref, keep_ref, cot_ref = refs[n_blocks + 1 + n_pieces : n_blocks + 4 + n_pieces]
    hid_ref, dg_ref, db_ref = refs[n_blocks + 4 + n_pieces : n_blocks + 7 + n_pieces]
    x_buf, w_buf, gate_buf, cell_buf, hid_buf, dg_buf, x_sem, w_sem, out_sem = refs[n_blocks + 7 + n_pieces :]
    time, width = x_buf.shape
    cols = gate_buf.shape[1]
    tile = w_buf.shape[2]
    def x_copy(i):
        start = pl.multiple_of(ids[at["time"] + i] * rows, rows)
        return pltpu.make_async_copy(x_refs[i], x_buf.at[pl.ds(start, rows), :], x_sem.at[i])

    def w_copies(col, size, slot):
        copies = []
        for i in range(n_pieces + 2):
            if i < 2:
                source = own_ref.at[i, :, pl.ds(offset + col, size)]
                block = ids[at["pieces"]] + i
            else:
                source = w_refs[i - 2].at[:, pl.ds(offset + col, size)]
                block = ids[at["pieces"] + i - 1]
            start = pl.multiple_of(block * half, half)
            copies.append(
                pltpu.make_async_copy(
                    source, w_buf.at[slot, pl.ds(start, half), pl.ds(0, size)], w_sem.at[slot, i]
                )
            )
        return copies

    full = cols // tile
    tail = cols - full * tile
    for i in range(n_blocks):
        x_copy(i).start()
    for copy in w_copies(0, tile, 0):
        copy.start()
    for i in range(n_blocks):
        x_copy(i).wait()
    row0 = lax.broadcasted_iota(jnp.int32, (time, 1), 0) == 0

    def product(slot, col, size):
        now = jnp.dot(x_buf[...], w_buf[slot, :width, :size], preferred_element_type=F32)
        prev = jnp.dot(x_buf[...], w_buf[slot, width:, :size], preferred_element_type=F32)
        prev = jnp.where(row0, 0.0, pltpu.roll(prev, 1, 0))
        gate_buf[:, pl.ds(col, size)] = now + prev + bias_ref[:, pl.ds(col, size)]

    @pl.loop(0, full)
    def _(n):
        slot = lax.rem(n, 2)

        @pl.when(n + 1 < full)
        def _():
            for copy in w_copies(pl.multiple_of((n + 1) * tile, tile), tile, 1 - slot):
                copy.start()

        if tail:

            @pl.when(n + 1 == full)
            def _():
                for copy in w_copies(full * tile, tail, 1 - slot):
                    copy.start()

        for copy in w_copies(pl.multiple_of(n * tile, tile), tile, slot):
            copy.wait()
        product(slot, pl.multiple_of(n * tile, tile), tile)

    if tail:
        for copy in w_copies(full * tile, tail, full % 2):
            copy.wait()
        product(full % 2, full * tile, tail)

    def out_copies(block):
        lane = block * LANES
        if not isinstance(block, int):
            lane = pl.multiple_of(lane, LANES)
        copies = [pltpu.make_async_copy(hid_buf.at[block], hid_ref.at[:, pl.ds(lane, LANES)], out_sem.at[block, 0])]
        for gate in range(3):
            copies.append(
                pltpu.make_async_copy(
                    dg_buf.at[block, :, :, pl.ds(gate * LANES, LANES)],
                    dg_ref.at[:, :, pl.ds(gate * group + lane, LANES)],
                    out_sem.at[block, 1 + gate],
                )
            )
        return copies

    scan(time, group, gate_buf, keep_ref, cot_ref, cell_buf, hid_buf, dg_buf, db_ref, out_copies)
    for block in range(group // LANES):
        for copy in out_copies(block):
            copy.wait()


STEP = 16


def scan(time, group, gate_buf, keep_ref, cot_ref, cell_buf, hid_buf, dg_buf, db_ref, out_copies):
    steps = time // STEP
    sub = lax.broadcasted_iota(jnp.int32, (8, LANES), 0)
    zeros = jnp.zeros((8, LANES), F32)

    def down(a, d):
        return pltpu.roll(a, d, 0)

    def up(a, d):
        return pltpu.roll(a, 8 - d, 0)

    def spread(a, r):
        return jnp.broadcast_to(a[r : r + 1, :], (8, LANES))

    @pl.loop(0, group // LANES)
    def _(block):
        lane = pl.multiple_of(block * LANES, LANES)
        z_at = pl.ds(lane, LANES)
        f_at = pl.ds(pl.multiple_of(group + lane, LANES), LANES)
        o_at = pl.ds(pl.multiple_of(2 * group + lane, LANES), LANES)

        def forward(i, carry):
            at = pl.multiple_of(i * STEP, STEP)
            outs = []
            for h in range(STEP // 8):
                here = pl.ds(at + 8 * h, 8)
                cand = jnp.tanh(gate_buf[here, z_at])
                forget = sigmoid(gate_buf[here, f_at])
                outgate = sigmoid(gate_buf[here, o_at])
                a = forget * keep_ref[here, :]
                b = (1.0 - forget) * cand
                gate_buf[here, z_at] = cand
                gate_buf[here, f_at] = forget
                gate_buf[here, o_at] = outgate
                for d in (1, 2, 4):
                    inside = sub >= d
                    b = b + a * jnp.where(inside, down(b, d), 0.0)
                    a = a * jnp.where(inside, down(a, d), 1.0)
                cell = b + a * carry
                carry = spread(b, 7) + spread(a, 7) * carry
                cell_buf[here, :] = cell
                outs.append(outgate * cell)
            hid_buf[block, pl.ds(at, STEP), :] = jnp.concatenate(outs, axis=0).astype(BF)
            return carry

        lax.fori_loop(0, steps, forward, zeros, unroll=16)

        def backward(n, state):
            adj_in, decay_in, later, total = state
            i = steps - 1 - n
            at = pl.multiple_of(i * STEP, STEP)
            grads = cot_ref[pl.ds(at, STEP), z_at].astype(F32)
            parts = []
            for h in reversed(range(STEP // 8)):
                here = pl.ds(at + 8 * h, 8)
                cand = gate_buf[here, z_at]
                forget = gate_buf[here, f_at]
                outgate = gate_buf[here, o_at]
                keep = keep_ref[here, :]
                cell = cell_buf[here, :]
                first = at + 8 * h == 0
                before = cell_buf[pl.ds(jnp.maximum(at + 8 * h - 8, 0), 8), :]
                before = jnp.where(first, 0.0, before)
                prev = jnp.where(sub == 0, down(before, 1), down(cell, 1))
                g = grads[8 * h : 8 * h + 8]
                decay = forget * keep
                a = jnp.where(sub == 7, decay_in, up(decay, 1))
                b = g * outgate
                for d in (1, 2, 4):
                    inside = sub < 8 - d
                    b = b + a * jnp.where(inside, up(b, d), 0.0)
                    a = a * jnp.where(inside, up(a, d), 1.0)
                adj = b + a * adj_in
                adj_in = spread(b, 0) + spread(a, 0) * adj_in
                decay_in = spread(decay, 0)
                omf = 1.0 - forget
                scaled = adj * omf
                d_z = scaled * (1.0 - cand * cand)
                d_f = scaled * forget * (keep * prev - cand)
                d_o = g * cell * (outgate * (1.0 - outgate))
                parts.append((d_z, d_f, d_o))
            parts.reverse()
            new_later, new_total = [], []
            for gate, where in enumerate((z_at, f_at, o_at)):
                tiles = [part[gate].astype(BF) for part in parts]
                wide = [t.astype(F32) for t in tiles]
                dg_buf[block, 0, pl.ds(at, STEP), gate * LANES : (gate + 1) * LANES] = jnp.concatenate(tiles, axis=0)
                follow = wide[1:] + [None]
                moved = []
                for t, nxt in zip(wide, follow):
                    edge = later[gate] if nxt is None else spread(nxt, 0)
                    moved.append(jnp.where(sub == 7, edge, up(t, 1)))
                dg_buf[block, 1, pl.ds(at, STEP), gate * LANES : (gate + 1) * LANES] = jnp.concatenate(moved, axis=0).astype(BF)
                new_later.append(spread(wide[0], 0))
                new_total.append(total[gate] + functools.reduce(jnp.add, wide))
            return adj_in, decay_in, tuple(new_later), tuple(new_total)

        triple = (zeros, zeros, zeros)
        _, _, _, total = lax.fori_loop(0, steps, backward, (zeros, zeros, triple, triple), unroll=8)
        for gate, where in enumerate((z_at, f_at, o_at)):
            db_ref[:, where] = total[gate]
        for copy in out_copies(block):
            copy.start()


def gates_call(at, ids, blocks, own, pieces, offset, bias, keep, cot, group):
    rows, width = blocks[0].shape
    half = own.shape[1]
    cols = 3 * group
    time = keep.shape[0]
    tile = min(256, cols)
    kernel = functools.partial(gates_kernel, at, rows, half, len(blocks), len(pieces), group, offset)
    return pl.pallas_call(
        kernel,
        out_shape=(
            jax.ShapeDtypeStruct((time, group), BF),
            jax.ShapeDtypeStruct((2, time, cols), BF),
            jax.ShapeDtypeStruct((8, cols), F32),
        ),
        in_specs=[smem_spec()]
        + [any_spec()] * (len(blocks) + 1 + len(pieces))
        + [vmem_spec()] * 3,
        out_specs=(any_spec(), any_spec(), vmem_spec()),
        scratch_shapes=[
            pltpu.VMEM((time, width), BF),
            pltpu.VMEM((2, 2 * width, tile), BF),
            pltpu.VMEM((time, cols), F32),
            pltpu.VMEM((time, LANES), F32),
            pltpu.VMEM((group // LANES, time, LANES), BF),
            pltpu.VMEM((group // LANES, 2, time, 3 * LANES), BF),
            pltpu.SemaphoreType.DMA((len(blocks),)),
            pltpu.SemaphoreType.DMA((2, len(pieces) + 2)),
            pltpu.SemaphoreType.DMA((group // LANES, 4)),
        ],
        compiler_params=pltpu.CompilerParams(vmem_limit_bytes=VMEM_BYTES),
        cost_estimate=cost(2 * time * 2 * width * cols * 1.5),
        name="gates",
    )(ids, *blocks, own, *pieces, bias, keep, cot)


def inputs_kernel(at_id, k, half, n_pieces, chunk, units, ids, *refs):
    dg_refs = refs[: len(units)]
    groups = 1 + max(g for g, _ in units)
    at = len(units) + groups * (n_pieces + 1)
    weights = [refs[len(units) + g * (n_pieces + 1) : len(units) + (g + 1) * (n_pieces + 1)] for g in range(groups)]
    out_ref = refs[at]
    w_buf, dg_buf, acc, w_sem, dg_sem = refs[at + 1 :]
    rows, width = acc.shape
    row = pl.multiple_of(ids[at_id["far"] + k] * rows, rows)

    def w_copies(g, col, size, slot):
        copies = []
        for i in range(n_pieces + 2):
            if i < 2:
                source = weights[g][0].at[i, :, pl.ds(col, size)]
                block = ids[at_id["pieces"]] + i
            else:
                source = weights[g][i - 1].at[:, pl.ds(col, size)]
                block = ids[at_id["pieces"] + i - 1]
            start = pl.multiple_of(block * half, half)
            copies.append(
                pltpu.make_async_copy(
                    source, w_buf.at[slot, pl.ds(start, half), pl.ds(0, size)], w_sem.at[slot, i]
                )
            )
        return copies

    firsts = [sum(ref.shape[2] for ref in dg_refs[:u]) for u in range(len(units))]

    def dg_copy(u):
        cols = dg_refs[u].shape[2]
        return pltpu.make_async_copy(
            dg_refs[u].at[:, pl.ds(row, rows), :], dg_buf.at[:, :, pl.ds(firsts[u], cols)], dg_sem.at[u]
        )

    jobs = []
    for u, (g, offset) in enumerate(units):
        cols = dg_refs[u].shape[2]
        for col in range(0, cols, chunk):
            jobs.append((u, col, (g, offset + col, min(chunk, cols - col))))
    step = 768 if width % 768 == 0 else LANES
    dg_copy(0).start()
    for copy in w_copies(*jobs[0][2], 0):
        copy.start()
    for u in range(1, len(units)):
        dg_copy(u).start()
    for n, (u, col, job) in enumerate(jobs):
        slot, size = n % 2, job[2]
        if n + 1 < len(jobs):
            for copy in w_copies(*jobs[n + 1][2], 1 - slot):
                copy.start()
        if col == 0:
            dg_copy(u).wait()
        for copy in w_copies(*job, slot):
            copy.wait()
        here = slice(firsts[u] + col, firsts[u] + col + size)

        @pl.loop(0, width // step)
        def _(k):
            at = pl.ds(pl.multiple_of(k * step, step), step)
            total = None if n == 0 else acc[:, at]
            for tap in range(2):
                feats = pl.ds(pl.multiple_of(tap * width + k * step, LANES), step)
                part = lax.dot_general(
                    dg_buf[tap, :, here],
                    w_buf[slot, feats, :size],
                    (((1,), (1,)), ((), ())),
                    preferred_element_type=F32,
                )
                total = part if total is None else total + part
            if n + 1 < len(jobs):
                acc[:, at] = total
            else:
                out_ref[:, at] = total.astype(out_ref.dtype)


def inputs_call(at, ids, k, dgs, weights, units, rows, width, dtype):
    n_pieces = len(weights[0]) - 1
    half = weights[0][0].shape[1]
    cols = sum(d.shape[2] for d in dgs)
    chunk = 768
    flat = [w for group in weights for w in group]
    return pl.pallas_call(
        functools.partial(inputs_kernel, at, k, half, n_pieces, chunk, units),
        out_shape=jax.ShapeDtypeStruct((rows, width), dtype),
        in_specs=[smem_spec()] + [any_spec()] * (len(dgs) + len(flat)),
        out_specs=vmem_spec(),
        scratch_shapes=[
            pltpu.VMEM((2, 2 * width, chunk), BF),
            pltpu.VMEM((2, rows, cols), BF),
            pltpu.VMEM((rows, width), F32),
            pltpu.SemaphoreType.DMA((2, n_pieces + 2)),
            pltpu.SemaphoreType.DMA((len(dgs),)),
        ],
        compiler_params=pltpu.CompilerParams(vmem_limit_bytes=VMEM_BYTES),
        cost_estimate=cost(2 * rows * 2 * width * cols),
        name="grad_in",
    )(ids, *dgs, *flat)


def turn_kernel(at, n_blocks, half, ids, *refs):
    x_refs, out_ref = refs[: 2 * n_blocks], refs[2 * n_blocks]
    x_buf, t_buf, sem = refs[2 * n_blocks + 1 :]
    rows = x_buf.shape[1]
    core = ids[at["core"]]
    jobs = [(i, m) for m in range(2) for i in range(n_blocks)]

    def load(n):
        return pltpu.make_async_copy(x_refs[n], x_buf.at[n % 2], sem.at[n % 2])

    load(0).start()
    for n, (i, m) in enumerate(jobs):
        if n + 1 < len(jobs):
            load(n + 1).start()
        load(n).wait()
        t_buf[...] = x_buf[n % 2].T
        column = pl.ds(pl.multiple_of(ids[at["time"] + i] * rows, rows), rows)
        for q in range(out_ref.shape[1]):
            start = pl.multiple_of(q * 2 * half + core * half, 16)
            out_ref[m, q, :, column] = t_buf[pl.ds(start, half), :]


def turn_call(at, ids, blocks, per_tap, half, time):
    rows, width = blocks[0].shape
    return pl.pallas_call(
        functools.partial(turn_kernel, at, len(blocks) // 2, half),
        out_shape=jax.ShapeDtypeStruct((2, per_tap, half, time), BF),
        in_specs=[smem_spec()] + [any_spec()] * len(blocks),
        out_specs=vmem_spec(),
        scratch_shapes=[
            pltpu.VMEM((2, rows, width), BF),
            pltpu.VMEM((width, rows), BF),
            pltpu.SemaphoreType.DMA((2,)),
        ],
        compiler_params=pltpu.CompilerParams(vmem_limit_bytes=VMEM_BYTES),
        cost_estimate=cost(7 * 10**9),
        name="turn",
    )(ids, *blocks)


def weight_kernel(count, offset, x_ref, *refs):
    mine_refs, other_refs, out_ref = refs[:count], refs[count : 2 * count], refs[-7]
    x_buf, dg_buf, out_buf, x_sem, in_sem, out_sem = refs[-6:]
    pieces, half, time = x_ref.shape[1:]
    jobs, col = [], offset
    for u in range(count):
        for tap in range(2):
            jobs.append((u, tap, col))
        col += mine_refs[u].shape[2]

    def x_copy(m):
        return pltpu.make_async_copy(x_ref.at[m], x_buf.at[m], x_sem.at[m])

    def dg_copies(n):
        u, tap, _ = jobs[n]
        size = mine_refs[u].shape[2]
        return [
            pltpu.make_async_copy(ref.at[tap], dg_buf.at[n % 2, m, :, pl.ds(0, size)], in_sem.at[n % 2, m])
            for m, ref in enumerate((mine_refs[u], other_refs[u]))
        ]

    def out_copy(n):
        u, tap, first = jobs[n]
        size = mine_refs[u].shape[2]
        return pltpu.make_async_copy(
            out_buf.at[n % 2, :, :, pl.ds(0, size)], out_ref.at[tap, :, :, pl.ds(first, size)], out_sem.at[n % 2]
        )

    x_copy(0).start()
    for copy in dg_copies(0):
        copy.start()
    x_copy(1).start()
    for n, (u, tap, first) in enumerate(jobs):
        size = mine_refs[u].shape[2]
        slot = n % 2
        if n + 1 < len(jobs):
            for copy in dg_copies(n + 1):
                copy.start()
        if n == 0:
            x_copy(0).wait()
            x_copy(1).wait()
        for copy in dg_copies(n):
            copy.wait()
        if n >= 2:
            out_copy(n - 2).wait()
        tile = 256 if size % 256 == 0 else LANES

        @pl.loop(0, size // tile)
        def _(k):
            at = pl.ds(pl.multiple_of(k * tile, tile), tile)
            total = None
            for m in range(2):
                part = jnp.dot(
                    x_buf[m].reshape(pieces * half, time), dg_buf[slot, m, :, at], preferred_element_type=F32
                )
                total = part if total is None else total + part
            out_buf[slot, :, :, at] = total.reshape(pieces, half, tile)

        out_copy(n).start()
    for n in range(max(0, len(jobs) - 2), len(jobs)):
        out_copy(n).wait()


def weight_call(x_t, mine, other, out, offset, width):
    _, pieces, half, time = x_t.shape
    cols = sum(d.shape[2] for d in mine)
    extra = [] if out is None else [out]
    most = max(d.shape[2] for d in mine)
    return pl.pallas_call(
        functools.partial(weight_kernel, len(mine), offset),
        out_shape=jax.ShapeDtypeStruct((2, pieces, half, width), F32),
        in_specs=[any_spec()] * (1 + 2 * len(mine) + len(extra)),
        input_output_aliases={1 + 2 * len(mine): 0} if extra else {},
        out_specs=any_spec(),
        scratch_shapes=[
            pltpu.VMEM(x_t.shape, BF),
            pltpu.VMEM((2, 2, time, most), BF),
            pltpu.VMEM((2, pieces, half, most), F32),
            pltpu.SemaphoreType.DMA((2,)),
            pltpu.SemaphoreType.DMA((2, 2)),
            pltpu.SemaphoreType.DMA((2,)),
        ],
        compiler_params=pltpu.CompilerParams(vmem_limit_bytes=VMEM_BYTES),
        cost_estimate=cost(8 * pieces * half * time * cols),
        name="grad_w",
    )(x_t, *mine, *other, *extra)


def place_kernel(at_id, count, spans, feats, width, ids, *refs):
    parts, out_ref = refs[:count], refs[-4]
    buf, in_sem, out_sem = refs[-3:]
    half = buf.shape[1]
    loads = [pltpu.make_async_copy(parts[i], buf.at[i], in_sem.at[i]) for i in range(count)]
    for copy in loads:
        copy.start()
    stores = []
    for i in range(count):
        loads[i].wait()
        row = pl.multiple_of(ids[at_id["place"] + 2 * i] * half, half)
        col = 0
        for start, size in spans:
            for gate in range(3):
                at = pl.multiple_of(gate * width + ids[at_id["place"] + 2 * i + 1] * feats + start, LANES)
                stores.append(
                    pltpu.make_async_copy(
                        buf.at[i, :, pl.ds(col, size)],
                        out_ref.at[pl.ds(row, half), pl.ds(at, size)],
                        out_sem.at[len(stores)],
                    )
                )
                stores[-1].start()
                col += size
    for copy in stores:
        copy.wait()


def place_call(at, ids, parts, out, spans, feats, rows, width):
    half, cols = parts[0].shape
    extra = [] if out is None else [out]
    return pl.pallas_call(
        functools.partial(place_kernel, at, len(parts), spans, feats, width),
        out_shape=jax.ShapeDtypeStruct((rows, 3 * width), F32),
        in_specs=[smem_spec()] + [any_spec()] * (len(parts) + len(extra)),
        out_specs=any_spec(),
        scratch_shapes=[
            pltpu.VMEM((len(parts), half, cols), F32),
            pltpu.SemaphoreType.DMA((len(parts),)),
            pltpu.SemaphoreType.DMA((3 * len(spans) * len(parts),)),
        ],
        input_output_aliases={1 + len(parts): 0} if extra else {},
        compiler_params=pltpu.CompilerParams(vmem_limit_bytes=VMEM_BYTES),
        cost_estimate=cost(5 * 10**9),
        name="place",
    )(ids, *parts, *extra)


def after(a, *others):
    return lax.optimization_barrier((a,) + others)[0] if others else a


class Links:
    def __init__(self):
        self.n_stream = lax.axis_size("stream")
        self.n_stretch = lax.axis_size("stretch")
        self.n_x = self.n_stretch // 2
        self.hops = self.n_stream // 2
        self.order = ring_order(self.n_stream)
        self.place_of = [self.order.index(i) for i in range(self.n_stream)]
        self.pairs = [self.ring_pairs(True), self.ring_pairs(False)]
        table = [self.numbers(s, p) for s in range(self.n_stretch) for p in range(self.n_stream)]
        self.at, total = {}, 0
        for name, numbers in table[0].items():
            self.at[name] = total
            total += len(numbers)
        flat = jnp.array(np.array([sum(row.values(), []) for row in table], np.int32))
        me = (lax.axis_index("stretch") * self.n_stream + lax.axis_index("stream")).astype(jnp.uint32)
        self.ids = lax.dynamic_index_in_dim(flat, me, 0, False)
        self.unsigned = self.ids.astype(jnp.uint32)
        self.x, self.c, self.p = (self.number(name) for name in ("x", "core", "stream"))

    def numbers(self, s, p):
        n, hops = self.n_stream, self.hops
        x, c, r = s // 2, s % 2, self.place_of[p]
        sign = 1 - 2 * c

        def owner(steps):
            return self.order[(r + sign * steps) % n]

        pieces = [2 * p]
        for t in range(1, hops + 1):
            pieces += [2 * owner(-t) + c, 2 * owner(t) + (1 - c)]
            if t < hops:
                pieces += [2 * owner(t) + c, 2 * owner(-t) + (1 - c)]
        far = [x ^ k for k in range(self.n_x)]
        return {
            "x": [x],
            "core": [c],
            "stream": [p],
            "time": [i * 2 + c for i in far] + [i * 2 + 1 - c for i in far],
            "pieces": pieces,
            "far": far,
            "place": [v for core in (c, 1 - c) for i in far for v in (core, i)],
            "forth": [owner(hops - t) for t in range(hops)],
            "back": [owner(t + 1 - hops) for t in range(hops - 1)],
        }

    def number(self, name, i=0):
        return self.unsigned[self.at[name] + i]

    def ring_pairs(self, forward):
        pairs = []
        for st in range(self.n_stretch):
            up = (st % 2 == 0) == forward
            for i in range(self.n_stream):
                j = (self.place_of[i] + (1 if up else -1)) % self.n_stream
                pairs.append((st * self.n_stream + i, st * self.n_stream + self.order[j]))
        return pairs

    def long(self, a):
        return lax.ppermute(a, ("stretch", "stream"), self.pairs[0])

    def short(self, a):
        return lax.ppermute(a, ("stretch", "stream"), self.pairs[1])

    def to_core(self, a):
        return lax.ppermute(a, "stretch", [(i, i ^ 1) for i in range(self.n_stretch)])

    def to_x(self, a, k):
        return lax.ppermute(a, "stretch", [(i, i ^ (2 * k)) for i in range(self.n_stretch)])

    def by_x(self, options):
        out = options[0]
        for i in range(1, self.n_x):
            out = jnp.where(self.x == i, options[i], out)
        return out

    def in_x_order(self, by_k):
        return [self.by_x([by_k[i ^ j] for j in range(self.n_x)]) for i in range(self.n_x)]

    def by_core(self, mine, other):
        return jnp.where(self.c == 0, mine, other), jnp.where(self.c == 0, other, mine)


class Gather:
    def __init__(self, links, mine):
        self.links = links
        self.forth = self.back = mine
        self.step = 0
        self.waiting, self.crossed, self.group, self.marks = [], [], [], []

    def cross(self, *deps):
        self.crossed = []
        for piece in self.waiting:
            self.crossed.append(self.links.to_core(after(piece, *deps)))
            self.group += [piece, self.crossed[-1]]
        self.waiting = []

    def hop(self, *deps, cross=True):
        links = self.links
        given, deps = deps, tuple(self.crossed) + deps
        self.step += 1
        forth, back, *_ = lax.optimization_barrier((self.forth, self.back) + deps)
        forth = links.long(forth)
        arriving = [forth]
        if self.step < links.hops:
            self.back = links.short(back)
            arriving.append(self.back)
            self.marks = arriving
        self.forth = forth
        if cross:
            self.cross(*given)
        self.waiting += arriving

    def hops_until(self, last, *deps):
        while self.step < last:
            self.hop(*deps)
            deps = ()


class Reduce:
    def __init__(self, links, local):
        self.links, self.local = links, local
        self.forth = self.back = None
        self.step = 0

    def part(self, shard, incoming):
        part = lax.dynamic_index_in_dim(self.local, shard, 0, False)
        part = part if incoming is None else part + incoming.astype(F32)
        return part.astype(BF)

    def hop(self, *deps):
        links, t = self.links, self.step
        self.step += 1
        if t:
            self.forth, self.back, *_ = lax.optimization_barrier((self.forth, self.back) + deps)
        else:
            self.local = after(self.local, *deps)
        sent = [self.part(links.number("forth", t), self.forth)]
        self.forth = links.long(sent[0])
        if t < links.hops - 1:
            sent.append(self.part(links.number("back", t), self.back))
            self.back = links.short(sent[1])
        return sent

    def hops_until(self, last, *deps):
        sent = []
        while self.step < last:
            sent = self.hop(*deps)
            deps = ()
        return sent

    def total(self, *deps):
        own = lax.dynamic_index_in_dim(self.local, self.links.p, 0, False)
        return own + after(self.forth, *deps).astype(F32) + self.back.astype(F32)


def shards(inputs, weight, bias, reset, cotangent):
    batches, _, rows, width = inputs.shape
    shard_rows, gate_cols = weight.shape
    links = Links()
    n_x, hops, x, c = links.n_x, links.hops, links.x, links.c
    at, ids = links.at, links.ids
    others_x = range(1, n_x)
    time = rows * links.n_stretch
    half = shard_rows // 2
    per_tap = links.n_stream // 2
    feats = width // n_x
    own_rows = time // n_x

    tiles = -(-feats // LANES)
    counts = [tiles // 5 + (1 if u in (0, 1, 3, 4)[: tiles % 5] else 0) for u in range(5)]
    sizes = [count * LANES for count in counts]
    starts = [sum(sizes[:u]) for u in range(5)]
    reals = [min(size, feats - start) for start, size in zip(starts, sizes)]
    members = [[0, 1], [2, 3, 4]]
    place_in_group = [(0, 0), (0, 3 * sizes[0])] + [(1, 3 * (starts[u] - starts[2])) for u in (2, 3, 4)]
    grad_members = [[0, 1, 2], [3, 4]]

    def columns(a, u):
        options = []
        for i in range(n_x):
            parts = []
            for gate in range(3):
                first_col = gate * width + i * feats + starts[u]
                part = a[..., first_col : first_col + reals[u]]
                if reals[u] < sizes[u]:
                    part = jnp.pad(part, [(0, 0)] * (a.ndim - 1) + [(0, sizes[u] - reals[u])])
                parts.append(part)
            options.append(jnp.concatenate(parts, axis=-1))
        return links.by_x(options)

    def halves(g, *deps):
        late = after(weight, *deps)
        parts = [columns(late, u) for u in members[g]]
        return jnp.concatenate(parts, axis=1).reshape(2, half, -1)

    def mine_of(own, *deps):
        return after(lax.dynamic_index_in_dim(own, c, 0, False), *deps)

    tokens = inputs.reshape(batches, rows, width)
    cots = cotangent.reshape(batches, rows, width)

    tok_mine = lax.dynamic_index_in_dim(tokens, c, 0, False)
    tok_away = lax.dynamic_index_in_dim(tokens, 1 - c, 0, False)
    x_mine = [links.to_x(tok_mine, k) for k in others_x]
    tok_pair = links.to_core(tok_away)
    x_pair = [links.to_x(tok_pair, k) for k in others_x]
    own_weights = [halves(0, tok_mine)]
    first = Gather(links, mine_of(own_weights[0]))
    first.hop()
    cot_mine = lax.dynamic_index_in_dim(cots, c, 0, False)
    cot_other = links.to_core(lax.dynamic_index_in_dim(cots, 1 - c, 0, False))
    reset_mine = reset.reshape(batches, rows).astype(F32)
    reset_pair = jnp.stack(links.by_core(reset_mine, links.to_core(reset_mine)), axis=1)
    first.hop()
    first.hops_until(hops - 2)
    first.hop(*x_mine, *x_pair)
    own_weights += [halves(1, *first.waiting)]
    blocks = [tok_mine] + x_mine + [tok_pair] + x_pair

    blocks_away = [tok_away] + [links.to_core(a) for a in x_pair]
    blocks_away += [links.to_core(tok_mine)] + [links.to_core(a) for a in x_mine]

    first.hop()
    second = Gather(links, mine_of(own_weights[1], *first.marks))

    cot_pair = jnp.concatenate(links.by_core(cot_mine, cot_other), axis=0)

    def cot_unit(u, *deps):
        parts = []
        for i in range(n_x):
            first_col = i * feats + starts[u]
            part = cot_pair[:, first_col : first_col + reals[u]]
            if reals[u] < sizes[u]:
                part = jnp.pad(part, [(0, 0), (0, sizes[u] - reals[u])])
            parts.append(part)
        by_k = [links.by_x(parts)]
        for k in others_x:
            leaving = links.by_x([parts[i ^ k] for i in range(n_x)])
            by_k.append(links.to_x(after(leaving, *deps), k))
        return jnp.concatenate(links.in_x_order(by_k), axis=0), by_k[1:]

    cot_units, cot_marks = [None] * 5, [None] * 5
    cot_units[0], cot_marks[0] = cot_unit(0)
    reset_parts = [reset_pair] + [after(links.to_x(reset_pair, k), *x_pair) for k in others_x]
    keep = jnp.stack(links.in_x_order(reset_parts), axis=1)
    keep = 1.0 - lax.dynamic_index_in_dim(keep, c, 0, False).reshape(time, 1)
    second.hop()
    first.cross()
    for u in range(1, 5):
        cot_units[u], cot_marks[u] = cot_unit(u, *x_pair)

    bias_units = [columns(bias[None, :], u) for u in range(5)]
    hiddens, dgs, others, biases = [], [], [], []

    def gates(u, gather, *deps):
        g, offset = place_in_group[u]
        hid, dg, db = gates_call(
            at, ids, blocks, after(own_weights[g], *deps), gather.group, offset, bias_units[u], keep, cot_units[u], sizes[u]
        )
        hiddens.append(hid[:, : reals[u]])
        dgs.append(dg)
        others.append(links.to_core(dg))
        biases.append(jnp.sum(db, axis=0).reshape(3, sizes[u])[:, : reals[u]])
        return db

    def local_gradient(units, out, offset, total, *deps):
        mine = [dgs[u] for u in units]
        mine[0] = after(mine[0], *deps)
        return weight_call(x_t, mine, [others[u] for u in units], out, offset, 3 * total)

    done = gates(0, first)
    arrived = second.waiting
    second.hop(done, *sum(cot_marks[1:], []), cross=False)
    done = gates(1, first)
    second.hops_until(hops - 2)
    second.hop(done)

    blocks_away[0] = after(blocks_away[0], done)

    if half % 16 == 0 and rows % LANES == 0:
        x_t = turn_call(at, ids, blocks + blocks_away, per_tap, half, time)
    else:
        x_t = []
        for group in (blocks, blocks_away):
            whole = jnp.zeros((time, width), BF)
            for i, block in enumerate(group):
                whole = lax.dynamic_update_slice(whole, block, (links.ids[at["time"] + i] * rows, 0))
            turned = whole.T.reshape(per_tap, 2, half, time)
            x_t.append(lax.dynamic_index_in_dim(turned, c, 1, False))
        x_t = jnp.stack(x_t)

    total = sum(sizes[:3])
    second.hop(x_t)
    second.cross()
    gates(2, second)
    done = gates(3, second)

    local = local_gradient([0, 1], None, 0, total, done)
    local = local_gradient([2], local, 3 * (sizes[0] + sizes[1]), total)
    red_first = Reduce(links, local.reshape(links.n_stream, half, -1))
    sent = red_first.hop()
    done = gates(4, second, *sent)
    sent = red_first.hops_until(hops - 2, done)

    hid = jnp.concatenate(hiddens, axis=1).reshape(n_x, own_rows, feats)
    pieces = [[own] + gather.group for own, gather in zip(own_weights, (first, second))]

    def d_inputs(k, dtype, *deps):
        now = [after(dgs[0], *deps)] + dgs[1:]
        return inputs_call(at, ids, k, now, pieces, place_in_group, own_rows, width, dtype)

    total = sum(sizes[3:])
    local = local_gradient([3], None, 0, total, *sent)
    local = local_gradient([4], local, 3 * sizes[3], total).reshape(links.n_stream, half, -1)
    red_last = Reduce(links, local)
    hid = after(hid, local)
    hid_by_k = [lax.dynamic_index_in_dim(hid, x, 0, False)]
    for k in others_x:
        hid_by_k.append(links.to_x(lax.dynamic_index_in_dim(hid, links.number("far", k), 0, False), k))
    hid = jnp.concatenate(links.in_x_order(hid_by_k), axis=1).reshape(2, rows, width)
    hid_mine = lax.dynamic_index_in_dim(hid, c, 0, False)
    hid_away = lax.dynamic_index_in_dim(hid, 1 - c, 0, False)

    sent = red_first.hop(local) + red_last.hop(local)
    d_others = [d_inputs(k, BF, *sent) for k in others_x]
    d_received = [links.to_x(a, k) for a, k in zip(d_others, others_x)]
    hid_other = links.to_core(after(hid_away, *d_others))
    hidden = jnp.stack(links.by_core(hid_mine, hid_other)).reshape(inputs.shape)
    sent = red_first.hop(*d_others, *hid_by_k[1:]) + red_last.hop(*d_others)
    d_mine = d_inputs(0, F32, *sent)

    aligned = feats % LANES == 0
    parts = [[None] * n_x for _ in sizes]

    def code(total):
        scale = jnp.maximum(jnp.max(jnp.abs(total), axis=0, keepdims=True), 1e-30) * 2.0**-15
        coded, scale = lax.optimization_barrier(((total / scale).astype(jnp.float16), scale))
        return coded, jnp.broadcast_to(scale, (8, scale.shape[1]))

    def spread(coded, scale, *deps):
        got = [(coded, scale)]
        got += [(after(links.to_x(coded, k), *deps), after(links.to_x(scale, k), *deps)) for k in others_x]
        values = [a.astype(F32) * b[:1] for a, b in got]
        return values, [links.to_core(a) for a in values]

    def put(grad_weight, units, got, crossed):
        spans = [(starts[u], sizes[u]) for u in units]
        if aligned:
            return place_call(at, ids, got + crossed, grad_weight, spans, feats, shard_rows, width)
        got = [jnp.concatenate(links.by_core(a, b), axis=0) for a, b in zip(got, crossed)]
        col = 0
        ordered = links.in_x_order(got)
        for u in units:
            for i in range(n_x):
                piece = ordered[i][:, col : col + 3 * sizes[u]]
                parts[u][i] = piece.reshape(shard_rows, 3, sizes[u])[:, :, : reals[u]]
            col += 3 * sizes[u]
        return None

    red_last.hops_until(hops - 2, d_mine)
    coded = code(red_first.total(d_mine))
    sent = red_last.hops_until(hops - 1, *d_received)
    got, crossed = spread(*coded, red_last.forth, red_last.back)
    red_last.hop()

    grad_weight = put(None, grad_members[0], got, crossed)
    for a in d_received:
        d_mine = d_mine + a.astype(F32)
    d_mine = d_mine.reshape(2, rows, width)
    d_keep = lax.dynamic_index_in_dim(d_mine, c, 0, False)
    d_other = links.to_core(lax.dynamic_index_in_dim(d_mine, 1 - c, 0, False))
    grad_inputs = jnp.stack(links.by_core(d_keep, d_other)).reshape(inputs.shape)
    red_last.forth, grad_inputs, hidden = lax.optimization_barrier((red_last.forth, grad_inputs, hidden))
    coded = code(red_last.total())

    bias_part = after(jnp.concatenate(biases, axis=1), *coded)
    bias_part = bias_part + links.to_core(bias_part)
    bit = 1
    while bit < links.n_stream:
        swaps = [(i, i ^ bit) for i in range(links.n_stream)]
        bias_part = bias_part + lax.ppermute(bias_part, "stream", swaps)
        bit *= 2
    bias_parts = [bias_part] + [links.to_x(bias_part, k) for k in others_x]
    grad_bias = jnp.stack(links.in_x_order(bias_parts), axis=1).reshape(gate_cols)

    got, crossed = spread(*coded, grad_bias, *([grad_weight] if aligned else []))
    grad_weight = put(grad_weight, grad_members[1], got, crossed)
    if not aligned:
        grad_weight = jnp.concatenate(
            [parts[u][i][:, gate] for gate in range(3) for i in range(n_x) for u in range(5)], axis=1
        )
    return (hidden, grad_inputs, grad_weight, grad_bias)


def solution(mesh):
    in_specs = (
        P(None, "stream", "stretch", None),
        P("stream", None),
        P(),
        P(None, "stream", "stretch"),
        P(None, "stream", "stretch", None),
    )
    out_specs = (
        P(None, "stream", "stretch", None),
        P(None, "stream", "stretch", None),
        P("stream", None),
        P(),
    )
    return jax.shard_map(shards, mesh=mesh, in_specs=in_specs, out_specs=out_specs, check_vma=False)
```

```python
import functools

import jax
import jax.numpy as jnp
import numpy as np
from jax import lax
from jax.experimental import pallas as pl
from jax.experimental.pallas import tpu as pltpu
from jax.sharding import PartitionSpec as P

BF = jnp.bfloat16
F32 = jnp.float32
LANES = 128
VMEM_BYTES = 60 * 1024 * 1024


def cost(flops):
    return pl.CostEstimate(flops=int(5 * flops), bytes_accessed=10**6, transcendentals=0)


def any_spec():
    return pl.BlockSpec(memory_space=pl.ANY)


def vmem_spec():
    return pl.BlockSpec(memory_space=pltpu.VMEM)


def smem_spec():
    return pl.BlockSpec(memory_space=pltpu.SMEM)


def ring_order(count):
    inner = 1
    while (2 * inner) ** 2 <= count:
        inner *= 2
    outer = count // inner
    if inner == 1 or outer % 2:
        return list(range(count))
    order = [z * inner for z in range(outer)]
    for turn, z in enumerate(reversed(range(outer))):
        across = range(1, inner) if turn % 2 == 0 else reversed(range(1, inner))
        order += [z * inner + y for y in across]
    return order


def sigmoid(v):
    return 0.5 + 0.5 * jnp.tanh(0.5 * v)


def gates_kernel(at, rows, half, n_blocks, n_pieces, group, offset, ids, *refs):
    x_refs = refs[:n_blocks]
    own_ref = refs[n_blocks]
    w_refs = refs[n_blocks + 1 : n_blocks + 1 + n_pieces]
    bias_ref, keep_ref, cot_ref = refs[n_blocks + 1 + n_pieces : n_blocks + 4 + n_pieces]
    hid_ref, dg_ref, db_ref = refs[n_blocks + 4 + n_pieces : n_blocks + 7 + n_pieces]
    x_buf, w_buf, gate_buf, cell_buf, hid_buf, dg_buf, x_sem, w_sem, out_sem = refs[n_blocks + 7 + n_pieces :]
    time, width = x_buf.shape
    cols = gate_buf.shape[1]
    tile = w_buf.shape[2]
    def x_copy(i):
        start = pl.multiple_of(ids[at["time"] + i] * rows, rows)
        return pltpu.make_async_copy(x_refs[i], x_buf.at[pl.ds(start, rows), :], x_sem.at[i])

    def w_copies(col, size, slot):
        copies = []
        for i in range(n_pieces + 2):
            if i < 2:
                source = own_ref.at[i, :, pl.ds(offset + col, size)]
                block = ids[at["pieces"]] + i
            else:
                source = w_refs[i - 2].at[:, pl.ds(offset + col, size)]
                block = ids[at["pieces"] + i - 1]
            start = pl.multiple_of(block * half, half)
            copies.append(
                pltpu.make_async_copy(
                    source, w_buf.at[slot, pl.ds(start, half), pl.ds(0, size)], w_sem.at[slot, i]
                )
            )
        return copies

    full = cols // tile
    tail = cols - full * tile
    for i in range(n_blocks):
        x_copy(i).start()
    for copy in w_copies(0, tile, 0):
        copy.start()
    for i in range(n_blocks):
        x_copy(i).wait()
    row0 = lax.broadcasted_iota(jnp.int32, (time, 1), 0) == 0

    def product(slot, col, size):
        now = jnp.dot(x_buf[...], w_buf[slot, :width, :size], preferred_element_type=F32)
        prev = jnp.dot(x_buf[...], w_buf[slot, width:, :size], preferred_element_type=F32)
        prev = jnp.where(row0, 0.0, pltpu.roll(prev, 1, 0))
        gate_buf[:, pl.ds(col, size)] = now + prev + bias_ref[:, pl.ds(col, size)]

    @pl.loop(0, full)
    def _(n):
        slot = lax.rem(n, 2)

        @pl.when(n + 1 < full)
        def _():
            for copy in w_copies(pl.multiple_of((n + 1) * tile, tile), tile, 1 - slot):
                copy.start()

        if tail:

            @pl.when(n + 1 == full)
            def _():
                for copy in w_copies(full * tile, tail, 1 - slot):
                    copy.start()

        for copy in w_copies(pl.multiple_of(n * tile, tile), tile, slot):
            copy.wait()
        product(slot, pl.multiple_of(n * tile, tile), tile)

    if tail:
        for copy in w_copies(full * tile, tail, full % 2):
            copy.wait()
        product(full % 2, full * tile, tail)

    def out_copies(block):
        lane = block * LANES
        if not isinstance(block, int):
            lane = pl.multiple_of(lane, LANES)
        copies = [pltpu.make_async_copy(hid_buf.at[block], hid_ref.at[:, pl.ds(lane, LANES)], out_sem.at[block, 0])]
        for gate in range(3):
            copies.append(
                pltpu.make_async_copy(
                    dg_buf.at[block, :, :, pl.ds(gate * LANES, LANES)],
                    dg_ref.at[:, :, pl.ds(gate * group + lane, LANES)],
                    out_sem.at[block, 1 + gate],
                )
            )
        return copies

    scan(time, group, gate_buf, keep_ref, cot_ref, cell_buf, hid_buf, dg_buf, db_ref, out_copies)
    for block in range(group // LANES):
        for copy in out_copies(block):
            copy.wait()


STEP = 16


def scan(time, group, gate_buf, keep_ref, cot_ref, cell_buf, hid_buf, dg_buf, db_ref, out_copies):
    steps = time // STEP
    sub = lax.broadcasted_iota(jnp.int32, (8, LANES), 0)
    zeros = jnp.zeros((8, LANES), F32)

    def down(a, d):
        return pltpu.roll(a, d, 0)

    def up(a, d):
        return pltpu.roll(a, 8 - d, 0)

    def spread(a, r):
        return jnp.broadcast_to(a[r : r + 1, :], (8, LANES))

    @pl.loop(0, group // LANES)
    def _(block):
        lane = pl.multiple_of(block * LANES, LANES)
        z_at = pl.ds(lane, LANES)
        f_at = pl.ds(pl.multiple_of(group + lane, LANES), LANES)
        o_at = pl.ds(pl.multiple_of(2 * group + lane, LANES), LANES)

        def forward(i, carry):
            at = pl.multiple_of(i * STEP, STEP)
            outs = []
            for h in range(STEP // 8):
                here = pl.ds(at + 8 * h, 8)
                cand = jnp.tanh(gate_buf[here, z_at])
                forget = sigmoid(gate_buf[here, f_at])
                outgate = sigmoid(gate_buf[here, o_at])
                a = forget * keep_ref[here, :]
                b = (1.0 - forget) * cand
                gate_buf[here, z_at] = cand
                gate_buf[here, f_at] = forget
                gate_buf[here, o_at] = outgate
                for d in (1, 2, 4):
                    inside = sub >= d
                    b = b + a * jnp.where(inside, down(b, d), 0.0)
                    a = a * jnp.where(inside, down(a, d), 1.0)
                cell = b + a * carry
                carry = spread(b, 7) + spread(a, 7) * carry
                cell_buf[here, :] = cell
                outs.append(outgate * cell)
            hid_buf[block, pl.ds(at, STEP), :] = jnp.concatenate(outs, axis=0).astype(BF)
            return carry

        lax.fori_loop(0, steps, forward, zeros, unroll=16)

        def backward(n, state):
            adj_in, decay_in, later, total = state
            i = steps - 1 - n
            at = pl.multiple_of(i * STEP, STEP)
            grads = cot_ref[pl.ds(at, STEP), z_at].astype(F32)
            parts = []
            for h in reversed(range(STEP // 8)):
                here = pl.ds(at + 8 * h, 8)
                cand = gate_buf[here, z_at]
                forget = gate_buf[here, f_at]
                outgate = gate_buf[here, o_at]
                keep = keep_ref[here, :]
                cell = cell_buf[here, :]
                first = at + 8 * h == 0
                before = cell_buf[pl.ds(jnp.maximum(at + 8 * h - 8, 0), 8), :]
                before = jnp.where(first, 0.0, before)
                prev = jnp.where(sub == 0, down(before, 1), down(cell, 1))
                g = grads[8 * h : 8 * h + 8]
                decay = forget * keep
                a = jnp.where(sub == 7, decay_in, up(decay, 1))
                b = g * outgate
                for d in (1, 2, 4):
                    inside = sub < 8 - d
                    b = b + a * jnp.where(inside, up(b, d), 0.0)
                    a = a * jnp.where(inside, up(a, d), 1.0)
                adj = b + a * adj_in
                adj_in = spread(b, 0) + spread(a, 0) * adj_in
                decay_in = spread(decay, 0)
                omf = 1.0 - forget
                scaled = adj * omf
                d_z = scaled * (1.0 - cand * cand)
                d_f = scaled * forget * (keep * prev - cand)
                d_o = g * cell * (outgate * (1.0 - outgate))
                parts.append((d_z, d_f, d_o))
            parts.reverse()
            new_later, new_total = [], []
            for gate, where in enumerate((z_at, f_at, o_at)):
                tiles = [part[gate].astype(BF) for part in parts]
                wide = [t.astype(F32) for t in tiles]
                dg_buf[block, 0, pl.ds(at, STEP), gate * LANES : (gate + 1) * LANES] = jnp.concatenate(tiles, axis=0)
                follow = wide[1:] + [None]
                moved = []
                for t, nxt in zip(wide, follow):
                    edge = later[gate] if nxt is None else spread(nxt, 0)
                    moved.append(jnp.where(sub == 7, edge, up(t, 1)))
                dg_buf[block, 1, pl.ds(at, STEP), gate * LANES : (gate + 1) * LANES] = jnp.concatenate(moved, axis=0).astype(BF)
                new_later.append(spread(wide[0], 0))
                new_total.append(total[gate] + functools.reduce(jnp.add, wide))
            return adj_in, decay_in, tuple(new_later), tuple(new_total)

        triple = (zeros, zeros, zeros)
        _, _, _, total = lax.fori_loop(0, steps, backward, (zeros, zeros, triple, triple), unroll=8)
        for gate, where in enumerate((z_at, f_at, o_at)):
            db_ref[:, where] = total[gate]
        for copy in out_copies(block):
            copy.start()


def gates_call(at, ids, blocks, own, pieces, offset, bias, keep, cot, group):
    rows, width = blocks[0].shape
    half = own.shape[1]
    cols = 3 * group
    time = keep.shape[0]
    tile = min(256, cols)
    kernel = functools.partial(gates_kernel, at, rows, half, len(blocks), len(pieces), group, offset)
    return pl.pallas_call(
        kernel,
        out_shape=(
            jax.ShapeDtypeStruct((time, group), BF),
            jax.ShapeDtypeStruct((2, time, cols), BF),
            jax.ShapeDtypeStruct((8, cols), F32),
        ),
        in_specs=[smem_spec()]
        + [any_spec()] * (len(blocks) + 1 + len(pieces))
        + [vmem_spec()] * 3,
        out_specs=(any_spec(), any_spec(), vmem_spec()),
        scratch_shapes=[
            pltpu.VMEM((time, width), BF),
            pltpu.VMEM((2, 2 * width, tile), BF),
            pltpu.VMEM((time, cols), F32),
            pltpu.VMEM((time, LANES), F32),
            pltpu.VMEM((group // LANES, time, LANES), BF),
            pltpu.VMEM((group // LANES, 2, time, 3 * LANES), BF),
            pltpu.SemaphoreType.DMA((len(blocks),)),
            pltpu.SemaphoreType.DMA((2, len(pieces) + 2)),
            pltpu.SemaphoreType.DMA((group // LANES, 4)),
        ],
        compiler_params=pltpu.CompilerParams(vmem_limit_bytes=VMEM_BYTES),
        cost_estimate=cost(2 * time * 2 * width * cols * 1.5),
        name="gates",
    )(ids, *blocks, own, *pieces, bias, keep, cot)


def inputs_kernel(at_id, k, half, n_pieces, chunk, units, ids, *refs):
    dg_refs = refs[: len(units)]
    groups = 1 + max(g for g, _ in units)
    at = len(units) + groups * (n_pieces + 1)
    weights = [refs[len(units) + g * (n_pieces + 1) : len(units) + (g + 1) * (n_pieces + 1)] for g in range(groups)]
    out_ref = refs[at]
    w_buf, dg_buf, acc, w_sem, dg_sem = refs[at + 1 :]
    rows, width = acc.shape
    row = pl.multiple_of(ids[at_id["far"] + k] * rows, rows)

    def w_copies(g, col, size, slot):
        copies = []
        for i in range(n_pieces + 2):
            if i < 2:
                source = weights[g][0].at[i, :, pl.ds(col, size)]
                block = ids[at_id["pieces"]] + i
            else:
                source = weights[g][i - 1].at[:, pl.ds(col, size)]
                block = ids[at_id["pieces"] + i - 1]
            start = pl.multiple_of(block * half, half)
            copies.append(
                pltpu.make_async_copy(
                    source, w_buf.at[slot, pl.ds(start, half), pl.ds(0, size)], w_sem.at[slot, i]
                )
            )
        return copies

    firsts = [sum(ref.shape[2] for ref in dg_refs[:u]) for u in range(len(units))]

    def dg_copy(u):
        cols = dg_refs[u].shape[2]
        return pltpu.make_async_copy(
            dg_refs[u].at[:, pl.ds(row, rows), :], dg_buf.at[:, :, pl.ds(firsts[u], cols)], dg_sem.at[u]
        )

    jobs = []
    for u, (g, offset) in enumerate(units):
        cols = dg_refs[u].shape[2]
        for col in range(0, cols, chunk):
            jobs.append((u, col, (g, offset + col, min(chunk, cols - col))))
    step = 768 if width % 768 == 0 else LANES
    dg_copy(0).start()
    for copy in w_copies(*jobs[0][2], 0):
        copy.start()
    for u in range(1, len(units)):
        dg_copy(u).start()
    for n, (u, col, job) in enumerate(jobs):
        slot, size = n % 2, job[2]
        if n + 1 < len(jobs):
            for copy in w_copies(*jobs[n + 1][2], 1 - slot):
                copy.start()
        if col == 0:
            dg_copy(u).wait()
        for copy in w_copies(*job, slot):
            copy.wait()
        here = slice(firsts[u] + col, firsts[u] + col + size)

        @pl.loop(0, width // step)
        def _(k):
            at = pl.ds(pl.multiple_of(k * step, step), step)
            total = None if n == 0 else acc[:, at]
            for tap in range(2):
                feats = pl.ds(pl.multiple_of(tap * width + k * step, LANES), step)
                part = lax.dot_general(
                    dg_buf[tap, :, here],
                    w_buf[slot, feats, :size],
                    (((1,), (1,)), ((), ())),
                    preferred_element_type=F32,
                )
                total = part if total is None else total + part
            if n + 1 < len(jobs):
                acc[:, at] = total
            else:
                out_ref[:, at] = total.astype(out_ref.dtype)


def inputs_call(at, ids, k, dgs, weights, units, rows, width, dtype):
    n_pieces = len(weights[0]) - 1
    half = weights[0][0].shape[1]
    cols = sum(d.shape[2] for d in dgs)
    chunk = 768
    flat = [w for group in weights for w in group]
    return pl.pallas_call(
        functools.partial(inputs_kernel, at, k, half, n_pieces, chunk, units),
        out_shape=jax.ShapeDtypeStruct((rows, width), dtype),
        in_specs=[smem_spec()] + [any_spec()] * (len(dgs) + len(flat)),
        out_specs=vmem_spec(),
        scratch_shapes=[
            pltpu.VMEM((2, 2 * width, chunk), BF),
            pltpu.VMEM((2, rows, cols), BF),
            pltpu.VMEM((rows, width), F32),
            pltpu.SemaphoreType.DMA((2, n_pieces + 2)),
            pltpu.SemaphoreType.DMA((len(dgs),)),
        ],
        compiler_params=pltpu.CompilerParams(vmem_limit_bytes=VMEM_BYTES),
        cost_estimate=cost(2 * rows * 2 * width * cols),
        name="grad_in",
    )(ids, *dgs, *flat)


def turn_kernel(at, n_blocks, half, ids, *refs):
    x_refs, out_ref = refs[: 2 * n_blocks], refs[2 * n_blocks]
    x_buf, t_buf, sem = refs[2 * n_blocks + 1 :]
    rows = x_buf.shape[1]
    core = ids[at["core"]]
    jobs = [(i, m) for m in range(2) for i in range(n_blocks)]

    def load(n):
        return pltpu.make_async_copy(x_refs[n], x_buf.at[n % 2], sem.at[n % 2])

    load(0).start()
    for n, (i, m) in enumerate(jobs):
        if n + 1 < len(jobs):
            load(n + 1).start()
        load(n).wait()
        t_buf[...] = x_buf[n % 2].T
        column = pl.ds(pl.multiple_of(ids[at["time"] + i] * rows, rows), rows)
        for q in range(out_ref.shape[1]):
            start = pl.multiple_of(q * 2 * half + core * half, 16)
            out_ref[m, q, :, column] = t_buf[pl.ds(start, half), :]


def turn_call(at, ids, blocks, per_tap, half, time):
    rows, width = blocks[0].shape
    return pl.pallas_call(
        functools.partial(turn_kernel, at, len(blocks) // 2, half),
        out_shape=jax.ShapeDtypeStruct((2, per_tap, half, time), BF),
        in_specs=[smem_spec()] + [any_spec()] * len(blocks),
        out_specs=vmem_spec(),
        scratch_shapes=[
            pltpu.VMEM((2, rows, width), BF),
            pltpu.VMEM((width, rows), BF),
            pltpu.SemaphoreType.DMA((2,)),
        ],
        compiler_params=pltpu.CompilerParams(vmem_limit_bytes=VMEM_BYTES),
        cost_estimate=cost(7 * 10**9),
        name="turn",
    )(ids, *blocks)


def weight_kernel(count, offset, x_ref, *refs):
    mine_refs, other_refs, out_ref = refs[:count], refs[count : 2 * count], refs[-7]
    x_buf, dg_buf, out_buf, x_sem, in_sem, out_sem = refs[-6:]
    pieces, half, time = x_ref.shape[1:]
    jobs, col = [], offset
    for u in range(count):
        for tap in range(2):
            jobs.append((u, tap, col))
        col += mine_refs[u].shape[2]

    def x_copy(m):
        return pltpu.make_async_copy(x_ref.at[m], x_buf.at[m], x_sem.at[m])

    def dg_copies(n):
        u, tap, _ = jobs[n]
        size = mine_refs[u].shape[2]
        return [
            pltpu.make_async_copy(ref.at[tap], dg_buf.at[n % 2, m, :, pl.ds(0, size)], in_sem.at[n % 2, m])
            for m, ref in enumerate((mine_refs[u], other_refs[u]))
        ]

    def out_copy(n):
        u, tap, first = jobs[n]
        size = mine_refs[u].shape[2]
        return pltpu.make_async_copy(
            out_buf.at[n % 2, :, :, pl.ds(0, size)], out_ref.at[tap, :, :, pl.ds(first, size)], out_sem.at[n % 2]
        )

    x_copy(0).start()
    for copy in dg_copies(0):
        copy.start()
    x_copy(1).start()
    for n, (u, tap, first) in enumerate(jobs):
        size = mine_refs[u].shape[2]
        slot = n % 2
        if n + 1 < len(jobs):
            for copy in dg_copies(n + 1):
                copy.start()
        if n == 0:
            x_copy(0).wait()
            x_copy(1).wait()
        for copy in dg_copies(n):
            copy.wait()
        if n >= 2:
            out_copy(n - 2).wait()
        tile = 256 if size % 256 == 0 else LANES

        @pl.loop(0, size // tile)
        def _(k):
            at = pl.ds(pl.multiple_of(k * tile, tile), tile)
            total = None
            for m in range(2):
                part = jnp.dot(
                    x_buf[m].reshape(pieces * half, time), dg_buf[slot, m, :, at], preferred_element_type=F32
                )
                total = part if total is None else total + part
            out_buf[slot, :, :, at] = total.reshape(pieces, half, tile)

        out_copy(n).start()
    for n in range(max(0, len(jobs) - 2), len(jobs)):
        out_copy(n).wait()


def weight_call(x_t, mine, other, out, offset, width):
    _, pieces, half, time = x_t.shape
    cols = sum(d.shape[2] for d in mine)
    extra = [] if out is None else [out]
    most = max(d.shape[2] for d in mine)
    return pl.pallas_call(
        functools.partial(weight_kernel, len(mine), offset),
        out_shape=jax.ShapeDtypeStruct((2, pieces, half, width), F32),
        in_specs=[any_spec()] * (1 + 2 * len(mine) + len(extra)),
        input_output_aliases={1 + 2 * len(mine): 0} if extra else {},
        out_specs=any_spec(),
        scratch_shapes=[
            pltpu.VMEM(x_t.shape, BF),
            pltpu.VMEM((2, 2, time, most), BF),
            pltpu.VMEM((2, pieces, half, most), F32),
            pltpu.SemaphoreType.DMA((2,)),
            pltpu.SemaphoreType.DMA((2, 2)),
            pltpu.SemaphoreType.DMA((2,)),
        ],
        compiler_params=pltpu.CompilerParams(vmem_limit_bytes=VMEM_BYTES),
        cost_estimate=cost(8 * pieces * half * time * cols),
        name="grad_w",
    )(x_t, *mine, *other, *extra)


def place_kernel(at_id, count, spans, feats, width, ids, *refs):
    parts, out_ref = refs[:count], refs[-4]
    buf, in_sem, out_sem = refs[-3:]
    half = buf.shape[1]
    loads = [pltpu.make_async_copy(parts[i], buf.at[i], in_sem.at[i]) for i in range(count)]
    for copy in loads:
        copy.start()
    stores = []
    for i in range(count):
        loads[i].wait()
        row = pl.multiple_of(ids[at_id["place"] + 2 * i] * half, half)
        col = 0
        for start, size in spans:
            for gate in range(3):
                at = pl.multiple_of(gate * width + ids[at_id["place"] + 2 * i + 1] * feats + start, LANES)
                stores.append(
                    pltpu.make_async_copy(
                        buf.at[i, :, pl.ds(col, size)],
                        out_ref.at[pl.ds(row, half), pl.ds(at, size)],
                        out_sem.at[len(stores)],
                    )
                )
                stores[-1].start()
                col += size
    for copy in stores:
        copy.wait()


def place_call(at, ids, parts, out, spans, feats, rows, width):
    half, cols = parts[0].shape
    extra = [] if out is None else [out]
    return pl.pallas_call(
        functools.partial(place_kernel, at, len(parts), spans, feats, width),
        out_shape=jax.ShapeDtypeStruct((rows, 3 * width), F32),
        in_specs=[smem_spec()] + [any_spec()] * (len(parts) + len(extra)),
        out_specs=any_spec(),
        scratch_shapes=[
            pltpu.VMEM((len(parts), half, cols), F32),
            pltpu.SemaphoreType.DMA((len(parts),)),
            pltpu.SemaphoreType.DMA((3 * len(spans) * len(parts),)),
        ],
        input_output_aliases={1 + len(parts): 0} if extra else {},
        compiler_params=pltpu.CompilerParams(vmem_limit_bytes=VMEM_BYTES),
        cost_estimate=cost(5 * 10**9),
        name="place",
    )(ids, *parts, *extra)


def after(a, *others):
    return lax.optimization_barrier((a,) + others)[0] if others else a


class Links:
    def __init__(self):
        self.n_stream = lax.axis_size("stream")
        self.n_stretch = lax.axis_size("stretch")
        self.n_x = self.n_stretch // 2
        self.hops = self.n_stream // 2
        self.order = ring_order(self.n_stream)
        self.place_of = [self.order.index(i) for i in range(self.n_stream)]
        self.pairs = [self.ring_pairs(True), self.ring_pairs(False)]
        table = [self.numbers(s, p) for s in range(self.n_stretch) for p in range(self.n_stream)]
        self.at, total = {}, 0
        for name, numbers in table[0].items():
            self.at[name] = total
            total += len(numbers)
        flat = jnp.array(np.array([sum(row.values(), []) for row in table], np.int32))
        me = (lax.axis_index("stretch") * self.n_stream + lax.axis_index("stream")).astype(jnp.uint32)
        self.ids = lax.dynamic_index_in_dim(flat, me, 0, False)
        self.unsigned = self.ids.astype(jnp.uint32)
        self.x, self.c, self.p = (self.number(name) for name in ("x", "core", "stream"))

    def numbers(self, s, p):
        n, hops = self.n_stream, self.hops
        x, c, r = s // 2, s % 2, self.place_of[p]
        sign = 1 - 2 * c

        def owner(steps):
            return self.order[(r + sign * steps) % n]

        pieces = [2 * p]
        for t in range(1, hops + 1):
            pieces += [2 * owner(-t) + c, 2 * owner(t) + (1 - c)]
            if t < hops:
                pieces += [2 * owner(t) + c, 2 * owner(-t) + (1 - c)]
        far = [x ^ k for k in range(self.n_x)]
        return {
            "x": [x],
            "core": [c],
            "stream": [p],
            "time": [i * 2 + c for i in far] + [i * 2 + 1 - c for i in far],
            "pieces": pieces,
            "far": far,
            "place": [v for core in (c, 1 - c) for i in far for v in (core, i)],
            "forth": [owner(hops - t) for t in range(hops)],
            "back": [owner(t + 1 - hops) for t in range(hops - 1)],
        }

    def number(self, name, i=0):
        return self.unsigned[self.at[name] + i]

    def ring_pairs(self, forward):
        pairs = []
        for st in range(self.n_stretch):
            up = (st % 2 == 0) == forward
            for i in range(self.n_stream):
                j = (self.place_of[i] + (1 if up else -1)) % self.n_stream
                pairs.append((st * self.n_stream + i, st * self.n_stream + self.order[j]))
        return pairs

    def long(self, a):
        return lax.ppermute(a, ("stretch", "stream"), self.pairs[0])

    def short(self, a):
        return lax.ppermute(a, ("stretch", "stream"), self.pairs[1])

    def to_core(self, a):
        return lax.ppermute(a, "stretch", [(i, i ^ 1) for i in range(self.n_stretch)])

    def to_x(self, a, k):
        return lax.ppermute(a, "stretch", [(i, i ^ (2 * k)) for i in range(self.n_stretch)])

    def by_x(self, options):
        out = options[0]
        for i in range(1, self.n_x):
            out = jnp.where(self.x == i, options[i], out)
        return out

    def in_x_order(self, by_k):
        return [self.by_x([by_k[i ^ j] for j in range(self.n_x)]) for i in range(self.n_x)]

    def by_core(self, mine, other):
        return jnp.where(self.c == 0, mine, other), jnp.where(self.c == 0, other, mine)


class Gather:
    def __init__(self, links, mine):
        self.links = links
        self.forth = self.back = mine
        self.step = 0
        self.waiting, self.crossed, self.group, self.marks = [], [], [], []

    def cross(self, *deps):
        self.crossed = []
        for piece in self.waiting:
            self.crossed.append(self.links.to_core(after(piece, *deps)))
            self.group += [piece, self.crossed[-1]]
        self.waiting = []

    def hop(self, *deps, cross=True):
        links = self.links
        given, deps = deps, tuple(self.crossed) + deps
        self.step += 1
        forth, back, *_ = lax.optimization_barrier((self.forth, self.back) + deps)
        forth = links.long(forth)
        arriving = [forth]
        if self.step < links.hops:
            self.back = links.short(back)
            arriving.append(self.back)
            self.marks = arriving
        self.forth = forth
        if cross:
            self.cross(*given)
        self.waiting += arriving

    def hops_until(self, last, *deps):
        while self.step < last:
            self.hop(*deps)
            deps = ()


class Reduce:
    def __init__(self, links, local):
        self.links, self.local = links, local
        self.forth = self.back = None
        self.step = 0

    def part(self, shard, incoming):
        part = lax.dynamic_index_in_dim(self.local, shard, 0, False)
        part = part if incoming is None else part + incoming.astype(F32)
        return part.astype(BF)

    def hop(self, *deps):
        links, t = self.links, self.step
        self.step += 1
        if t:
            self.forth, self.back, *_ = lax.optimization_barrier((self.forth, self.back) + deps)
        else:
            self.local = after(self.local, *deps)
        sent = [self.part(links.number("forth", t), self.forth)]
        self.forth = links.long(sent[0])
        if t < links.hops - 1:
            sent.append(self.part(links.number("back", t), self.back))
            self.back = links.short(sent[1])
        return sent

    def hops_until(self, last, *deps):
        sent = []
        while self.step < last:
            sent = self.hop(*deps)
            deps = ()
        return sent

    def total(self, *deps):
        own = lax.dynamic_index_in_dim(self.local, self.links.p, 0, False)
        return own + after(self.forth, *deps).astype(F32) + self.back.astype(F32)


def shards(inputs, weight, bias, reset, cotangent):
    batches, _, rows, width = inputs.shape
    shard_rows, gate_cols = weight.shape
    links = Links()
    n_x, hops, x, c = links.n_x, links.hops, links.x, links.c
    at, ids = links.at, links.ids
    others_x = range(1, n_x)
    time = rows * links.n_stretch
    half = shard_rows // 2
    per_tap = links.n_stream // 2
    feats = width // n_x
    own_rows = time // n_x

    tiles = -(-feats // LANES)
    counts = [tiles // 5 + (1 if u in (0, 1, 3, 4)[: tiles % 5] else 0) for u in range(5)]
    sizes = [count * LANES for count in counts]
    starts = [sum(sizes[:u]) for u in range(5)]
    reals = [min(size, feats - start) for start, size in zip(starts, sizes)]
    members = [[0, 1], [2, 3, 4]]
    place_in_group = [(0, 0), (0, 3 * sizes[0])] + [(1, 3 * (starts[u] - starts[2])) for u in (2, 3, 4)]
    grad_members = [[0, 1, 2], [3, 4]]

    def columns(a, u):
        options = []
        for i in range(n_x):
            parts = []
            for gate in range(3):
                first_col = gate * width + i * feats + starts[u]
                part = a[..., first_col : first_col + reals[u]]
                if reals[u] < sizes[u]:
                    part = jnp.pad(part, [(0, 0)] * (a.ndim - 1) + [(0, sizes[u] - reals[u])])
                parts.append(part)
            options.append(jnp.concatenate(parts, axis=-1))
        return links.by_x(options)

    def halves(g, *deps):
        late = after(weight, *deps)
        parts = [columns(late, u) for u in members[g]]
        return jnp.concatenate(parts, axis=1).reshape(2, half, -1)

    def mine_of(own, *deps):
        return after(lax.dynamic_index_in_dim(own, c, 0, False), *deps)

    tokens = inputs.reshape(batches, rows, width)
    cots = cotangent.reshape(batches, rows, width)

    tok_mine = lax.dynamic_index_in_dim(tokens, c, 0, False)
    tok_away = lax.dynamic_index_in_dim(tokens, 1 - c, 0, False)
    x_mine = [links.to_x(tok_mine, k) for k in others_x]
    tok_pair = links.to_core(tok_away)
    x_pair = [links.to_x(tok_pair, k) for k in others_x]
    own_weights = [halves(0, tok_mine)]
    first = Gather(links, mine_of(own_weights[0]))
    first.hop()
    cot_mine = lax.dynamic_index_in_dim(cots, c, 0, False)
    cot_other = links.to_core(lax.dynamic_index_in_dim(cots, 1 - c, 0, False))
    reset_mine = reset.reshape(batches, rows).astype(F32)
    reset_pair = jnp.stack(links.by_core(reset_mine, links.to_core(reset_mine)), axis=1)
    first.hop()
    first.hops_until(hops - 2)
    first.hop(*x_mine)
    own_weights += [halves(1, *first.waiting)]
    blocks = [tok_mine] + x_mine + [tok_pair] + x_pair

    blocks_away = [tok_away] + [links.to_core(a) for a in x_pair]
    blocks_away += [links.to_core(tok_mine)] + [links.to_core(a) for a in x_mine]

    first.hop(*x_pair)
    second = Gather(links, mine_of(own_weights[1], *first.marks))

    cot_pair = jnp.concatenate(links.by_core(cot_mine, cot_other), axis=0)

    def cot_unit(u, *deps):
        parts = []
        for i in range(n_x):
            first_col = i * feats + starts[u]
            part = cot_pair[:, first_col : first_col + reals[u]]
            if reals[u] < sizes[u]:
                part = jnp.pad(part, [(0, 0), (0, sizes[u] - reals[u])])
            parts.append(part)
        by_k = [links.by_x(parts)]
        for k in others_x:
            leaving = links.by_x([parts[i ^ k] for i in range(n_x)])
            by_k.append(links.to_x(after(leaving, *deps), k))
        return jnp.concatenate(links.in_x_order(by_k), axis=0), by_k[1:]

    cot_units, cot_marks = [None] * 5, [None] * 5
    cot_units[0], cot_marks[0] = cot_unit(0)
    reset_parts = [reset_pair] + [after(links.to_x(reset_pair, k), *x_pair) for k in others_x]
    keep = jnp.stack(links.in_x_order(reset_parts), axis=1)
    keep = 1.0 - lax.dynamic_index_in_dim(keep, c, 0, False).reshape(time, 1)
    second.hop()
    first.cross()
    for u in range(1, 5):
        cot_units[u], cot_marks[u] = cot_unit(u, *x_pair)

    bias_units = [columns(bias[None, :], u) for u in range(5)]
    hiddens, dgs, others, biases = [], [], [], []

    def gates(u, gather, *deps):
        g, offset = place_in_group[u]
        hid, dg, db = gates_call(
            at, ids, blocks, after(own_weights[g], *deps), gather.group, offset, bias_units[u], keep, cot_units[u], sizes[u]
        )
        hiddens.append(hid[:, : reals[u]])
        dgs.append(dg)
        others.append(links.to_core(dg))
        biases.append(jnp.sum(db, axis=0).reshape(3, sizes[u])[:, : reals[u]])
        return db

    def local_gradient(units, out, offset, total, *deps):
        mine = [dgs[u] for u in units]
        mine[0] = after(mine[0], *deps)
        return weight_call(x_t, mine, [others[u] for u in units], out, offset, 3 * total)

    done = gates(0, first)
    arrived = second.waiting
    second.hop(done, *sum(cot_marks[1:], []), cross=False)
    done = gates(1, first)
    second.hops_until(hops - 2)
    second.hop(done)

    blocks_away[0] = after(blocks_away[0], done)

    if half % 16 == 0 and rows % LANES == 0:
        x_t = turn_call(at, ids, blocks + blocks_away, per_tap, half, time)
    else:
        x_t = []
        for group in (blocks, blocks_away):
            whole = jnp.zeros((time, width), BF)
            for i, block in enumerate(group):
                whole = lax.dynamic_update_slice(whole, block, (links.ids[at["time"] + i] * rows, 0))
            turned = whole.T.reshape(per_tap, 2, half, time)
            x_t.append(lax.dynamic_index_in_dim(turned, c, 1, False))
        x_t = jnp.stack(x_t)

    total = sum(sizes[:3])
    second.hop(x_t)
    second.cross()
    gates(2, second)
    done = gates(3, second)

    local = local_gradient([0, 1], None, 0, total, done)
    local = local_gradient([2], local, 3 * (sizes[0] + sizes[1]), total)
    red_first = Reduce(links, local.reshape(links.n_stream, half, -1))
    sent = red_first.hop()
    done = gates(4, second, *sent)
    sent = red_first.hops_until(hops - 2, done)

    hid = jnp.concatenate(hiddens, axis=1).reshape(n_x, own_rows, feats)
    pieces = [[own] + gather.group for own, gather in zip(own_weights, (first, second))]

    def d_inputs(k, dtype, *deps):
        now = [after(dgs[0], *deps)] + dgs[1:]
        return inputs_call(at, ids, k, now, pieces, place_in_group, own_rows, width, dtype)

    total = sum(sizes[3:])
    local = local_gradient([3], None, 0, total, *sent)
    local = local_gradient([4], local, 3 * sizes[3], total).reshape(links.n_stream, half, -1)
    red_last = Reduce(links, local)
    hid = after(hid, local)
    hid_by_k = [lax.dynamic_index_in_dim(hid, x, 0, False)]
    for k in others_x:
        hid_by_k.append(links.to_x(lax.dynamic_index_in_dim(hid, links.number("far", k), 0, False), k))
    hid = jnp.concatenate(links.in_x_order(hid_by_k), axis=1).reshape(2, rows, width)
    hid_mine = lax.dynamic_index_in_dim(hid, c, 0, False)
    hid_away = lax.dynamic_index_in_dim(hid, 1 - c, 0, False)

    sent = red_first.hop(local) + red_last.hop(local)
    d_others = [d_inputs(k, BF, *sent) for k in others_x]
    d_received = [links.to_x(a, k) for a, k in zip(d_others, others_x)]
    hid_other = links.to_core(after(hid_away, *d_others))
    hidden = jnp.stack(links.by_core(hid_mine, hid_other)).reshape(inputs.shape)
    sent = red_first.hop(*d_others, *hid_by_k[1:]) + red_last.hop(*d_others)
    d_mine = d_inputs(0, F32, *sent)

    aligned = feats % LANES == 0
    parts = [[None] * n_x for _ in sizes]

    def code(total):
        scale = jnp.maximum(jnp.max(jnp.abs(total), axis=0, keepdims=True), 1e-30) * 2.0**-15
        coded, scale = lax.optimization_barrier(((total / scale).astype(jnp.float16), scale))
        return coded, jnp.broadcast_to(scale, (8, scale.shape[1]))

    def spread(coded, scale, *deps):
        got = [(coded, scale)]
        got += [(after(links.to_x(coded, k), *deps), after(links.to_x(scale, k), *deps)) for k in others_x]
        values = [a.astype(F32) * b[:1] for a, b in got]
        return values, [links.to_core(a) for a in values]

    def put(grad_weight, units, got, crossed):
        spans = [(starts[u], sizes[u]) for u in units]
        if aligned:
            return place_call(at, ids, got + crossed, grad_weight, spans, feats, shard_rows, width)
        got = [jnp.concatenate(links.by_core(a, b), axis=0) for a, b in zip(got, crossed)]
        col = 0
        ordered = links.in_x_order(got)
        for u in units:
            for i in range(n_x):
                piece = ordered[i][:, col : col + 3 * sizes[u]]
                parts[u][i] = piece.reshape(shard_rows, 3, sizes[u])[:, :, : reals[u]]
            col += 3 * sizes[u]
        return None

    red_last.hops_until(hops - 2, d_mine)
    coded = code(red_first.total(d_mine))
    sent = red_last.hops_until(hops - 1, *d_received)
    got, crossed = spread(*coded, red_last.forth, red_last.back)
    red_last.hop()

    grad_weight = put(None, grad_members[0], got, crossed)
    for a in d_received:
        d_mine = d_mine + a.astype(F32)
    d_mine = d_mine.reshape(2, rows, width)
    d_keep = lax.dynamic_index_in_dim(d_mine, c, 0, False)
    d_other = links.to_core(lax.dynamic_index_in_dim(d_mine, 1 - c, 0, False))
    grad_inputs = jnp.stack(links.by_core(d_keep, d_other)).reshape(inputs.shape)
    red_last.forth, grad_inputs, hidden = lax.optimization_barrier((red_last.forth, grad_inputs, hidden))
    coded = code(red_last.total())

    bias_part = after(jnp.concatenate(biases, axis=1), *coded)
    bias_part = bias_part + links.to_core(bias_part)
    bit = 1
    while bit < links.n_stream:
        swaps = [(i, i ^ bit) for i in range(links.n_stream)]
        bias_part = bias_part + lax.ppermute(bias_part, "stream", swaps)
        bit *= 2
    bias_parts = [bias_part] + [links.to_x(bias_part, k) for k in others_x]
    grad_bias = jnp.stack(links.in_x_order(bias_parts), axis=1).reshape(gate_cols)

    got, crossed = spread(*coded, grad_bias, *([grad_weight] if aligned else []))
    grad_weight = put(grad_weight, grad_members[1], got, crossed)
    if not aligned:
        grad_weight = jnp.concatenate(
            [parts[u][i][:, gate] for gate in range(3) for i in range(n_x) for u in range(5)], axis=1
        )
    return (hidden, grad_inputs, grad_weight, grad_bias)


def solution(mesh):
    in_specs = (
        P(None, "stream", "stretch", None),
        P("stream", None),
        P(),
        P(None, "stream", "stretch"),
        P(None, "stream", "stretch", None),
    )
    out_specs = (
        P(None, "stream", "stretch", None),
        P(None, "stream", "stretch", None),
        P("stream", None),
        P(),
    )
    return jax.shard_map(shards, mesh=mesh, in_specs=in_specs, out_specs=out_specs, check_vma=False)
```

```python
import functools

import jax
import jax.numpy as jnp
import numpy as np
from jax import lax
from jax.experimental import pallas as pl
from jax.experimental.pallas import tpu as pltpu
from jax.sharding import PartitionSpec as P

BF = jnp.bfloat16
F32 = jnp.float32
LANES = 128
VMEM_BYTES = 60 * 1024 * 1024


def cost(flops):
    return pl.CostEstimate(flops=int(5 * flops), bytes_accessed=10**6, transcendentals=0)


def any_spec():
    return pl.BlockSpec(memory_space=pl.ANY)


def vmem_spec():
    return pl.BlockSpec(memory_space=pltpu.VMEM)


def smem_spec():
    return pl.BlockSpec(memory_space=pltpu.SMEM)


def ring_order(count):
    inner = 1
    while (2 * inner) ** 2 <= count:
        inner *= 2
    outer = count // inner
    if inner == 1 or outer % 2:
        return list(range(count))
    order = [z * inner for z in range(outer)]
    for turn, z in enumerate(reversed(range(outer))):
        across = range(1, inner) if turn % 2 == 0 else reversed(range(1, inner))
        order += [z * inner + y for y in across]
    return order


def sigmoid(v):
    return 0.5 + 0.5 * jnp.tanh(0.5 * v)


def gates_kernel(at, rows, half, n_blocks, n_pieces, group, offset, ids, *refs):
    x_refs = refs[:n_blocks]
    own_ref = refs[n_blocks]
    w_refs = refs[n_blocks + 1 : n_blocks + 1 + n_pieces]
    bias_ref, keep_ref, cot_ref = refs[n_blocks + 1 + n_pieces : n_blocks + 4 + n_pieces]
    hid_ref, dg_ref, db_ref = refs[n_blocks + 4 + n_pieces : n_blocks + 7 + n_pieces]
    x_buf, w_buf, gate_buf, cell_buf, hid_buf, dg_buf, x_sem, w_sem, out_sem = refs[n_blocks + 7 + n_pieces :]
    time, width = x_buf.shape
    cols = gate_buf.shape[1]
    tile = w_buf.shape[2]
    def x_copy(i):
        start = pl.multiple_of(ids[at["time"] + i] * rows, rows)
        return pltpu.make_async_copy(x_refs[i], x_buf.at[pl.ds(start, rows), :], x_sem.at[i])

    def w_copies(col, size, slot):
        copies = []
        for i in range(n_pieces + 2):
            if i < 2:
                source = own_ref.at[i, :, pl.ds(offset + col, size)]
                block = ids[at["pieces"]] + i
            else:
                source = w_refs[i - 2].at[:, pl.ds(offset + col, size)]
                block = ids[at["pieces"] + i - 1]
            start = pl.multiple_of(block * half, half)
            copies.append(
                pltpu.make_async_copy(
                    source, w_buf.at[slot, pl.ds(start, half), pl.ds(0, size)], w_sem.at[slot, i]
                )
            )
        return copies

    full = cols // tile
    tail = cols - full * tile
    for i in range(n_blocks):
        x_copy(i).start()
    for copy in w_copies(0, tile, 0):
        copy.start()
    for i in range(n_blocks):
        x_copy(i).wait()
    row0 = lax.broadcasted_iota(jnp.int32, (time, 1), 0) == 0

    def product(slot, col, size):
        now = jnp.dot(x_buf[...], w_buf[slot, :width, :size], preferred_element_type=F32)
        prev = jnp.dot(x_buf[...], w_buf[slot, width:, :size], preferred_element_type=F32)
        prev = jnp.where(row0, 0.0, pltpu.roll(prev, 1, 0))
        gate_buf[:, pl.ds(col, size)] = now + prev + bias_ref[:, pl.ds(col, size)]

    @pl.loop(0, full)
    def _(n):
        slot = lax.rem(n, 2)

        @pl.when(n + 1 < full)
        def _():
            for copy in w_copies(pl.multiple_of((n + 1) * tile, tile), tile, 1 - slot):
                copy.start()

        if tail:

            @pl.when(n + 1 == full)
            def _():
                for copy in w_copies(full * tile, tail, 1 - slot):
                    copy.start()

        for copy in w_copies(pl.multiple_of(n * tile, tile), tile, slot):
            copy.wait()
        product(slot, pl.multiple_of(n * tile, tile), tile)

    if tail:
        for copy in w_copies(full * tile, tail, full % 2):
            copy.wait()
        product(full % 2, full * tile, tail)

    def out_copies(block):
        lane = block * LANES
        if not isinstance(block, int):
            lane = pl.multiple_of(lane, LANES)
        copies = [pltpu.make_async_copy(hid_buf.at[block], hid_ref.at[:, pl.ds(lane, LANES)], out_sem.at[block, 0])]
        for gate in range(3):
            copies.append(
                pltpu.make_async_copy(
                    dg_buf.at[block, :, :, pl.ds(gate * LANES, LANES)],
                    dg_ref.at[:, :, pl.ds(gate * group + lane, LANES)],
                    out_sem.at[block, 1 + gate],
                )
            )
        return copies

    scan(time, group, gate_buf, keep_ref, cot_ref, cell_buf, hid_buf, dg_buf, db_ref, out_copies)
    for block in range(group // LANES):
        for copy in out_copies(block):
            copy.wait()


STEP = 16


def scan(time, group, gate_buf, keep_ref, cot_ref, cell_buf, hid_buf, dg_buf, db_ref, out_copies):
    steps = time // STEP
    sub = lax.broadcasted_iota(jnp.int32, (8, LANES), 0)
    zeros = jnp.zeros((8, LANES), F32)

    def down(a, d):
        return pltpu.roll(a, d, 0)

    def up(a, d):
        return pltpu.roll(a, 8 - d, 0)

    def spread(a, r):
        return jnp.broadcast_to(a[r : r + 1, :], (8, LANES))

    @pl.loop(0, group // LANES)
    def _(block):
        lane = pl.multiple_of(block * LANES, LANES)
        z_at = pl.ds(lane, LANES)
        f_at = pl.ds(pl.multiple_of(group + lane, LANES), LANES)
        o_at = pl.ds(pl.multiple_of(2 * group + lane, LANES), LANES)

        def forward(i, carry):
            at = pl.multiple_of(i * STEP, STEP)
            outs = []
            for h in range(STEP // 8):
                here = pl.ds(at + 8 * h, 8)
                cand = jnp.tanh(gate_buf[here, z_at])
                forget = sigmoid(gate_buf[here, f_at])
                outgate = sigmoid(gate_buf[here, o_at])
                a = forget * keep_ref[here, :]
                b = (1.0 - forget) * cand
                gate_buf[here, z_at] = cand
                gate_buf[here, f_at] = forget
                gate_buf[here, o_at] = outgate
                for d in (1, 2, 4):
                    inside = sub >= d
                    b = b + a * jnp.where(inside, down(b, d), 0.0)
                    a = a * jnp.where(inside, down(a, d), 1.0)
                cell = b + a * carry
                carry = spread(b, 7) + spread(a, 7) * carry
                cell_buf[here, :] = cell
                outs.append(outgate * cell)
            hid_buf[block, pl.ds(at, STEP), :] = jnp.concatenate(outs, axis=0).astype(BF)
            return carry

        lax.fori_loop(0, steps, forward, zeros, unroll=16)

        def backward(n, state):
            adj_in, decay_in, later, total = state
            i = steps - 1 - n
            at = pl.multiple_of(i * STEP, STEP)
            grads = cot_ref[pl.ds(at, STEP), z_at].astype(F32)
            parts = []
            for h in reversed(range(STEP // 8)):
                here = pl.ds(at + 8 * h, 8)
                cand = gate_buf[here, z_at]
                forget = gate_buf[here, f_at]
                outgate = gate_buf[here, o_at]
                keep = keep_ref[here, :]
                cell = cell_buf[here, :]
                first = at + 8 * h == 0
                before = cell_buf[pl.ds(jnp.maximum(at + 8 * h - 8, 0), 8), :]
                before = jnp.where(first, 0.0, before)
                prev = jnp.where(sub == 0, down(before, 1), down(cell, 1))
                g = grads[8 * h : 8 * h + 8]
                decay = forget * keep
                a = jnp.where(sub == 7, decay_in, up(decay, 1))
                b = g * outgate
                for d in (1, 2, 4):
                    inside = sub < 8 - d
                    b = b + a * jnp.where(inside, up(b, d), 0.0)
                    a = a * jnp.where(inside, up(a, d), 1.0)
                adj = b + a * adj_in
                adj_in = spread(b, 0) + spread(a, 0) * adj_in
                decay_in = spread(decay, 0)
                omf = 1.0 - forget
                scaled = adj * omf
                d_z = scaled * (1.0 - cand * cand)
                d_f = scaled * forget * (keep * prev - cand)
                d_o = g * cell * (outgate * (1.0 - outgate))
                parts.append((d_z, d_f, d_o))
            parts.reverse()
            new_later, new_total = [], []
            for gate, where in enumerate((z_at, f_at, o_at)):
                tiles = [part[gate].astype(BF) for part in parts]
                wide = [t.astype(F32) for t in tiles]
                dg_buf[block, 0, pl.ds(at, STEP), gate * LANES : (gate + 1) * LANES] = jnp.concatenate(tiles, axis=0)
                follow = wide[1:] + [None]
                moved = []
                for t, nxt in zip(wide, follow):
                    edge = later[gate] if nxt is None else spread(nxt, 0)
                    moved.append(jnp.where(sub == 7, edge, up(t, 1)))
                dg_buf[block, 1, pl.ds(at, STEP), gate * LANES : (gate + 1) * LANES] = jnp.concatenate(moved, axis=0).astype(BF)
                new_later.append(spread(wide[0], 0))
                new_total.append(total[gate] + functools.reduce(jnp.add, wide))
            return adj_in, decay_in, tuple(new_later), tuple(new_total)

        triple = (zeros, zeros, zeros)
        _, _, _, total = lax.fori_loop(0, steps, backward, (zeros, zeros, triple, triple), unroll=8)
        for gate, where in enumerate((z_at, f_at, o_at)):
            db_ref[:, where] = total[gate]
        for copy in out_copies(block):
            copy.start()


def gates_call(at, ids, blocks, own, pieces, offset, bias, keep, cot, group):
    rows, width = blocks[0].shape
    half = own.shape[1]
    cols = 3 * group
    time = keep.shape[0]
    tile = min(256, cols)
    kernel = functools.partial(gates_kernel, at, rows, half, len(blocks), len(pieces), group, offset)
    return pl.pallas_call(
        kernel,
        out_shape=(
            jax.ShapeDtypeStruct((time, group), BF),
            jax.ShapeDtypeStruct((2, time, cols), BF),
            jax.ShapeDtypeStruct((8, cols), F32),
        ),
        in_specs=[smem_spec()]
        + [any_spec()] * (len(blocks) + 1 + len(pieces))
        + [vmem_spec()] * 3,
        out_specs=(any_spec(), any_spec(), vmem_spec()),
        scratch_shapes=[
            pltpu.VMEM((time, width), BF),
            pltpu.VMEM((2, 2 * width, tile), BF),
            pltpu.VMEM((time, cols), F32),
            pltpu.VMEM((time, LANES), F32),
            pltpu.VMEM((group // LANES, time, LANES), BF),
            pltpu.VMEM((group // LANES, 2, time, 3 * LANES), BF),
            pltpu.SemaphoreType.DMA((len(blocks),)),
            pltpu.SemaphoreType.DMA((2, len(pieces) + 2)),
            pltpu.SemaphoreType.DMA((group // LANES, 4)),
        ],
        compiler_params=pltpu.CompilerParams(vmem_limit_bytes=VMEM_BYTES),
        cost_estimate=cost(2 * time * 2 * width * cols * 1.5),
        name="gates",
    )(ids, *blocks, own, *pieces, bias, keep, cot)


def inputs_kernel(at_id, k, half, n_pieces, chunk, units, ids, *refs):
    dg_refs = refs[: len(units)]
    groups = 1 + max(g for g, _ in units)
    at = len(units) + groups * (n_pieces + 1)
    weights = [refs[len(units) + g * (n_pieces + 1) : len(units) + (g + 1) * (n_pieces + 1)] for g in range(groups)]
    out_ref = refs[at]
    w_buf, dg_buf, acc, w_sem, dg_sem = refs[at + 1 :]
    rows, width = acc.shape
    row = pl.multiple_of(ids[at_id["far"] + k] * rows, rows)

    def w_copies(g, col, size, slot):
        copies = []
        for i in range(n_pieces + 2):
            if i < 2:
                source = weights[g][0].at[i, :, pl.ds(col, size)]
                block = ids[at_id["pieces"]] + i
            else:
                source = weights[g][i - 1].at[:, pl.ds(col, size)]
                block = ids[at_id["pieces"] + i - 1]
            start = pl.multiple_of(block * half, half)
            copies.append(
                pltpu.make_async_copy(
                    source, w_buf.at[slot, pl.ds(start, half), pl.ds(0, size)], w_sem.at[slot, i]
                )
            )
        return copies

    firsts = [sum(ref.shape[2] for ref in dg_refs[:u]) for u in range(len(units))]

    def dg_copy(u):
        cols = dg_refs[u].shape[2]
        return pltpu.make_async_copy(
            dg_refs[u].at[:, pl.ds(row, rows), :], dg_buf.at[:, :, pl.ds(firsts[u], cols)], dg_sem.at[u]
        )

    jobs = []
    for u, (g, offset) in enumerate(units):
        cols = dg_refs[u].shape[2]
        for col in range(0, cols, chunk):
            jobs.append((u, col, (g, offset + col, min(chunk, cols - col))))
    step = 768 if width % 768 == 0 else LANES
    dg_copy(0).start()
    for copy in w_copies(*jobs[0][2], 0):
        copy.start()
    for u in range(1, len(units)):
        dg_copy(u).start()
    for n, (u, col, job) in enumerate(jobs):
        slot, size = n % 2, job[2]
        if n + 1 < len(jobs):
            for copy in w_copies(*jobs[n + 1][2], 1 - slot):
                copy.start()
        if col == 0:
            dg_copy(u).wait()
        for copy in w_copies(*job, slot):
            copy.wait()
        here = slice(firsts[u] + col, firsts[u] + col + size)

        @pl.loop(0, width // step)
        def _(k):
            at = pl.ds(pl.multiple_of(k * step, step), step)
            total = None if n == 0 else acc[:, at]
            for tap in range(2):
                feats = pl.ds(pl.multiple_of(tap * width + k * step, LANES), step)
                part = lax.dot_general(
                    dg_buf[tap, :, here],
                    w_buf[slot, feats, :size],
                    (((1,), (1,)), ((), ())),
                    preferred_element_type=F32,
                )
                total = part if total is None else total + part
            if n + 1 < len(jobs):
                acc[:, at] = total
            else:
                out_ref[:, at] = total.astype(out_ref.dtype)


def inputs_call(at, ids, k, dgs, weights, units, rows, width, dtype):
    n_pieces = len(weights[0]) - 1
    half = weights[0][0].shape[1]
    cols = sum(d.shape[2] for d in dgs)
    chunk = 768
    flat = [w for group in weights for w in group]
    return pl.pallas_call(
        functools.partial(inputs_kernel, at, k, half, n_pieces, chunk, units),
        out_shape=jax.ShapeDtypeStruct((rows, width), dtype),
        in_specs=[smem_spec()] + [any_spec()] * (len(dgs) + len(flat)),
        out_specs=vmem_spec(),
        scratch_shapes=[
            pltpu.VMEM((2, 2 * width, chunk), BF),
            pltpu.VMEM((2, rows, cols), BF),
            pltpu.VMEM((rows, width), F32),
            pltpu.SemaphoreType.DMA((2, n_pieces + 2)),
            pltpu.SemaphoreType.DMA((len(dgs),)),
        ],
        compiler_params=pltpu.CompilerParams(vmem_limit_bytes=VMEM_BYTES),
        cost_estimate=cost(2 * rows * 2 * width * cols),
        name="grad_in",
    )(ids, *dgs, *flat)


def turn_kernel(at, n_blocks, half, ids, *refs):
    x_refs, out_ref = refs[: 2 * n_blocks], refs[2 * n_blocks]
    x_buf, t_buf, sem = refs[2 * n_blocks + 1 :]
    rows = x_buf.shape[1]
    core = ids[at["core"]]
    jobs = [(i, m) for m in range(2) for i in range(n_blocks)]

    def load(n):
        return pltpu.make_async_copy(x_refs[n], x_buf.at[n % 2], sem.at[n % 2])

    load(0).start()
    for n, (i, m) in enumerate(jobs):
        if n + 1 < len(jobs):
            load(n + 1).start()
        load(n).wait()
        t_buf[...] = x_buf[n % 2].T
        column = pl.ds(pl.multiple_of(ids[at["time"] + i] * rows, rows), rows)
        for q in range(out_ref.shape[1]):
            start = pl.multiple_of(q * 2 * half + core * half, 16)
            out_ref[m, q, :, column] = t_buf[pl.ds(start, half), :]


def turn_call(at, ids, blocks, per_tap, half, time):
    rows, width = blocks[0].shape
    return pl.pallas_call(
        functools.partial(turn_kernel, at, len(blocks) // 2, half),
        out_shape=jax.ShapeDtypeStruct((2, per_tap, half, time), BF),
        in_specs=[smem_spec()] + [any_spec()] * len(blocks),
        out_specs=vmem_spec(),
        scratch_shapes=[
            pltpu.VMEM((2, rows, width), BF),
            pltpu.VMEM((width, rows), BF),
            pltpu.SemaphoreType.DMA((2,)),
        ],
        compiler_params=pltpu.CompilerParams(vmem_limit_bytes=VMEM_BYTES),
        cost_estimate=cost(7 * 10**9),
        name="turn",
    )(ids, *blocks)


def weight_kernel(count, offset, x_ref, *refs):
    mine_refs, other_refs, out_ref = refs[:count], refs[count : 2 * count], refs[-7]
    x_buf, dg_buf, out_buf, x_sem, in_sem, out_sem = refs[-6:]
    pieces, half, time = x_ref.shape[1:]
    jobs, col = [], offset
    for u in range(count):
        for tap in range(2):
            jobs.append((u, tap, col))
        col += mine_refs[u].shape[2]

    def x_copy(m):
        return pltpu.make_async_copy(x_ref.at[m], x_buf.at[m], x_sem.at[m])

    def dg_copies(n):
        u, tap, _ = jobs[n]
        size = mine_refs[u].shape[2]
        return [
            pltpu.make_async_copy(ref.at[tap], dg_buf.at[n % 2, m, :, pl.ds(0, size)], in_sem.at[n % 2, m])
            for m, ref in enumerate((mine_refs[u], other_refs[u]))
        ]

    def out_copy(n):
        u, tap, first = jobs[n]
        size = mine_refs[u].shape[2]
        return pltpu.make_async_copy(
            out_buf.at[n % 2, :, :, pl.ds(0, size)], out_ref.at[tap, :, :, pl.ds(first, size)], out_sem.at[n % 2]
        )

    x_copy(0).start()
    for copy in dg_copies(0):
        copy.start()
    x_copy(1).start()
    for n, (u, tap, first) in enumerate(jobs):
        size = mine_refs[u].shape[2]
        slot = n % 2
        if n + 1 < len(jobs):
            for copy in dg_copies(n + 1):
                copy.start()
        if n == 0:
            x_copy(0).wait()
            x_copy(1).wait()
        for copy in dg_copies(n):
            copy.wait()
        if n >= 2:
            out_copy(n - 2).wait()
        tile = 256 if size % 256 == 0 else LANES

        @pl.loop(0, size // tile)
        def _(k):
            at = pl.ds(pl.multiple_of(k * tile, tile), tile)
            total = None
            for m in range(2):
                part = jnp.dot(
                    x_buf[m].reshape(pieces * half, time), dg_buf[slot, m, :, at], preferred_element_type=F32
                )
                total = part if total is None else total + part
            out_buf[slot, :, :, at] = total.reshape(pieces, half, tile)

        out_copy(n).start()
    for n in range(max(0, len(jobs) - 2), len(jobs)):
        out_copy(n).wait()


def weight_call(x_t, mine, other, out, offset, width):
    _, pieces, half, time = x_t.shape
    cols = sum(d.shape[2] for d in mine)
    extra = [] if out is None else [out]
    most = max(d.shape[2] for d in mine)
    return pl.pallas_call(
        functools.partial(weight_kernel, len(mine), offset),
        out_shape=jax.ShapeDtypeStruct((2, pieces, half, width), F32),
        in_specs=[any_spec()] * (1 + 2 * len(mine) + len(extra)),
        input_output_aliases={1 + 2 * len(mine): 0} if extra else {},
        out_specs=any_spec(),
        scratch_shapes=[
            pltpu.VMEM(x_t.shape, BF),
            pltpu.VMEM((2, 2, time, most), BF),
            pltpu.VMEM((2, pieces, half, most), F32),
            pltpu.SemaphoreType.DMA((2,)),
            pltpu.SemaphoreType.DMA((2, 2)),
            pltpu.SemaphoreType.DMA((2,)),
        ],
        compiler_params=pltpu.CompilerParams(vmem_limit_bytes=VMEM_BYTES),
        cost_estimate=cost(8 * pieces * half * time * cols),
        name="grad_w",
    )(x_t, *mine, *other, *extra)


def place_kernel(at_id, count, spans, feats, width, ids, *refs):
    parts, out_ref = refs[:count], refs[-4]
    buf, in_sem, out_sem = refs[-3:]
    half = buf.shape[1]
    loads = [pltpu.make_async_copy(parts[i], buf.at[i], in_sem.at[i]) for i in range(count)]
    for copy in loads:
        copy.start()
    stores = []
    for i in range(count):
        loads[i].wait()
        row = pl.multiple_of(ids[at_id["place"] + 2 * i] * half, half)
        col = 0
        for start, size in spans:
            for gate in range(3):
                at = pl.multiple_of(gate * width + ids[at_id["place"] + 2 * i + 1] * feats + start, LANES)
                stores.append(
                    pltpu.make_async_copy(
                        buf.at[i, :, pl.ds(col, size)],
                        out_ref.at[pl.ds(row, half), pl.ds(at, size)],
                        out_sem.at[len(stores)],
                    )
                )
                stores[-1].start()
                col += size
    for copy in stores:
        copy.wait()


def place_call(at, ids, parts, out, spans, feats, rows, width):
    half, cols = parts[0].shape
    extra = [] if out is None else [out]
    return pl.pallas_call(
        functools.partial(place_kernel, at, len(parts), spans, feats, width),
        out_shape=jax.ShapeDtypeStruct((rows, 3 * width), F32),
        in_specs=[smem_spec()] + [any_spec()] * (len(parts) + len(extra)),
        out_specs=any_spec(),
        scratch_shapes=[
            pltpu.VMEM((len(parts), half, cols), F32),
            pltpu.SemaphoreType.DMA((len(parts),)),
            pltpu.SemaphoreType.DMA((3 * len(spans) * len(parts),)),
        ],
        input_output_aliases={1 + len(parts): 0} if extra else {},
        compiler_params=pltpu.CompilerParams(vmem_limit_bytes=VMEM_BYTES),
        cost_estimate=cost(5 * 10**9),
        name="place",
    )(ids, *parts, *extra)


def after(a, *others):
    return lax.optimization_barrier((a,) + others)[0] if others else a


class Links:
    def __init__(self):
        self.n_stream = lax.axis_size("stream")
        self.n_stretch = lax.axis_size("stretch")
        self.n_x = self.n_stretch // 2
        self.hops = self.n_stream // 2
        self.order = ring_order(self.n_stream)
        self.place_of = [self.order.index(i) for i in range(self.n_stream)]
        self.pairs = [self.ring_pairs(True), self.ring_pairs(False)]
        table = [self.numbers(s, p) for s in range(self.n_stretch) for p in range(self.n_stream)]
        self.at, total = {}, 0
        for name, numbers in table[0].items():
            self.at[name] = total
            total += len(numbers)
        flat = jnp.array(np.array([sum(row.values(), []) for row in table], np.int32))
        me = (lax.axis_index("stretch") * self.n_stream + lax.axis_index("stream")).astype(jnp.uint32)
        self.ids = lax.dynamic_index_in_dim(flat, me, 0, False)
        self.unsigned = self.ids.astype(jnp.uint32)
        self.x, self.c, self.p = (self.number(name) for name in ("x", "core", "stream"))

    def numbers(self, s, p):
        n, hops = self.n_stream, self.hops
        x, c, r = s // 2, s % 2, self.place_of[p]
        sign = 1 - 2 * c

        def owner(steps):
            return self.order[(r + sign * steps) % n]

        pieces = [2 * p]
        for t in range(1, hops + 1):
            pieces += [2 * owner(-t) + c, 2 * owner(t) + (1 - c)]
            if t < hops:
                pieces += [2 * owner(t) + c, 2 * owner(-t) + (1 - c)]
        far = [x ^ k for k in range(self.n_x)]
        return {
            "x": [x],
            "core": [c],
            "stream": [p],
            "time": [i * 2 + c for i in far] + [i * 2 + 1 - c for i in far],
            "pieces": pieces,
            "far": far,
            "place": [v for core in (c, 1 - c) for i in far for v in (core, i)],
            "forth": [owner(hops - t) for t in range(hops)],
            "back": [owner(t + 1 - hops) for t in range(hops - 1)],
        }

    def number(self, name, i=0):
        return self.unsigned[self.at[name] + i]

    def ring_pairs(self, forward):
        pairs = []
        for st in range(self.n_stretch):
            up = (st % 2 == 0) == forward
            for i in range(self.n_stream):
                j = (self.place_of[i] + (1 if up else -1)) % self.n_stream
                pairs.append((st * self.n_stream + i, st * self.n_stream + self.order[j]))
        return pairs

    def long(self, a):
        return lax.ppermute(a, ("stretch", "stream"), self.pairs[0])

    def short(self, a):
        return lax.ppermute(a, ("stretch", "stream"), self.pairs[1])

    def to_core(self, a):
        return lax.ppermute(a, "stretch", [(i, i ^ 1) for i in range(self.n_stretch)])

    def to_x(self, a, k):
        return lax.ppermute(a, "stretch", [(i, i ^ (2 * k)) for i in range(self.n_stretch)])

    def by_x(self, options):
        out = options[0]
        for i in range(1, self.n_x):
            out = jnp.where(self.x == i, options[i], out)
        return out

    def in_x_order(self, by_k):
        return [self.by_x([by_k[i ^ j] for j in range(self.n_x)]) for i in range(self.n_x)]

    def by_core(self, mine, other):
        return jnp.where(self.c == 0, mine, other), jnp.where(self.c == 0, other, mine)


class Gather:
    def __init__(self, links, mine):
        self.links = links
        self.forth = self.back = mine
        self.step = 0
        self.waiting, self.crossed, self.group, self.marks = [], [], [], []

    def cross(self, *deps):
        self.crossed = []
        for piece in self.waiting:
            self.crossed.append(self.links.to_core(after(piece, *deps)))
            self.group += [piece, self.crossed[-1]]
        self.waiting = []

    def hop(self, *deps, cross=True):
        links = self.links
        given, deps = deps, tuple(self.crossed) + deps
        self.step += 1
        forth, back, *_ = lax.optimization_barrier((self.forth, self.back) + deps)
        forth = links.long(forth)
        arriving = [forth]
        if self.step < links.hops:
            self.back = links.short(back)
            arriving.append(self.back)
            self.marks = arriving
        self.forth = forth
        if cross:
            self.cross(*given)
        self.waiting += arriving

    def hops_until(self, last, *deps):
        while self.step < last:
            self.hop(*deps)
            deps = ()


class Reduce:
    def __init__(self, links, local):
        self.links, self.local = links, local
        self.forth = self.back = None
        self.step = 0

    def part(self, shard, incoming):
        part = lax.dynamic_index_in_dim(self.local, shard, 0, False)
        part = part if incoming is None else part + incoming.astype(F32)
        return part.astype(BF)

    def hop(self, *deps):
        links, t = self.links, self.step
        self.step += 1
        if t:
            self.forth, self.back, *_ = lax.optimization_barrier((self.forth, self.back) + deps)
        else:
            self.local = after(self.local, *deps)
        sent = [self.part(links.number("forth", t), self.forth)]
        self.forth = links.long(sent[0])
        if t < links.hops - 1:
            sent.append(self.part(links.number("back", t), self.back))
            self.back = links.short(sent[1])
        return sent

    def hops_until(self, last, *deps):
        sent = []
        while self.step < last:
            sent = self.hop(*deps)
            deps = ()
        return sent

    def total(self, *deps):
        own = lax.dynamic_index_in_dim(self.local, self.links.p, 0, False)
        return own + after(self.forth, *deps).astype(F32) + self.back.astype(F32)


def shards(inputs, weight, bias, reset, cotangent):
    batches, _, rows, width = inputs.shape
    shard_rows, gate_cols = weight.shape
    links = Links()
    n_x, hops, x, c = links.n_x, links.hops, links.x, links.c
    at, ids = links.at, links.ids
    others_x = range(1, n_x)
    time = rows * links.n_stretch
    half = shard_rows // 2
    per_tap = links.n_stream // 2
    feats = width // n_x
    own_rows = time // n_x

    tiles = -(-feats // LANES)
    counts = [tiles // 5 + (1 if u in (0, 1, 3, 4)[: tiles % 5] else 0) for u in range(5)]
    sizes = [count * LANES for count in counts]
    starts = [sum(sizes[:u]) for u in range(5)]
    reals = [min(size, feats - start) for start, size in zip(starts, sizes)]
    members = [[0, 1], [2, 3, 4]]
    place_in_group = [(0, 0), (0, 3 * sizes[0])] + [(1, 3 * (starts[u] - starts[2])) for u in (2, 3, 4)]
    grad_members = [[0, 1, 2], [3, 4]]

    def columns(a, u):
        options = []
        for i in range(n_x):
            parts = []
            for gate in range(3):
                first_col = gate * width + i * feats + starts[u]
                part = a[..., first_col : first_col + reals[u]]
                if reals[u] < sizes[u]:
                    part = jnp.pad(part, [(0, 0)] * (a.ndim - 1) + [(0, sizes[u] - reals[u])])
                parts.append(part)
            options.append(jnp.concatenate(parts, axis=-1))
        return links.by_x(options)

    def halves(g, *deps):
        late = after(weight, *deps)
        parts = [columns(late, u) for u in members[g]]
        return jnp.concatenate(parts, axis=1).reshape(2, half, -1)

    def mine_of(own, *deps):
        return after(lax.dynamic_index_in_dim(own, c, 0, False), *deps)

    tokens = inputs.reshape(batches, rows, width)
    cots = cotangent.reshape(batches, rows, width)

    tok_mine = lax.dynamic_index_in_dim(tokens, c, 0, False)
    tok_away = lax.dynamic_index_in_dim(tokens, 1 - c, 0, False)
    x_mine = [links.to_x(tok_mine, k) for k in others_x]
    tok_pair = links.to_core(tok_away)
    x_pair = [links.to_x(tok_pair, k) for k in others_x]
    own_weights = [halves(0, tok_mine)]
    first = Gather(links, mine_of(own_weights[0]))
    first.hop()
    cot_mine = lax.dynamic_index_in_dim(cots, c, 0, False)
    cot_other = links.to_core(lax.dynamic_index_in_dim(cots, 1 - c, 0, False))
    reset_mine = reset.reshape(batches, rows).astype(F32)
    reset_pair = jnp.stack(links.by_core(reset_mine, links.to_core(reset_mine)), axis=1)
    first.hop()
    first.hops_until(hops - 2)
    first.hop(*x_mine)
    own_weights += [halves(1, *first.waiting)]
    blocks = [tok_mine] + x_mine + [tok_pair] + x_pair

    blocks_away = [tok_away] + [links.to_core(a) for a in x_pair]
    blocks_away += [links.to_core(tok_mine)] + [links.to_core(a) for a in x_mine]

    first.hop(*x_pair)
    second = Gather(links, mine_of(own_weights[1], *first.marks))

    cot_pair = jnp.concatenate(links.by_core(cot_mine, cot_other), axis=0)

    def cot_unit(u, *deps):
        parts = []
        for i in range(n_x):
            first_col = i * feats + starts[u]
            part = cot_pair[:, first_col : first_col + reals[u]]
            if reals[u] < sizes[u]:
                part = jnp.pad(part, [(0, 0), (0, sizes[u] - reals[u])])
            parts.append(part)
        by_k = [links.by_x(parts)]
        for k in others_x:
            leaving = links.by_x([parts[i ^ k] for i in range(n_x)])
            by_k.append(links.to_x(after(leaving, *deps), k))
        return jnp.concatenate(links.in_x_order(by_k), axis=0), by_k[1:]

    cot_units, cot_marks = [None] * 5, [None] * 5
    cot_units[0], cot_marks[0] = cot_unit(0)
    reset_parts = [reset_pair] + [after(links.to_x(reset_pair, k), *x_pair) for k in others_x]
    keep = jnp.stack(links.in_x_order(reset_parts), axis=1)
    keep = 1.0 - lax.dynamic_index_in_dim(keep, c, 0, False).reshape(time, 1)
    second.hop()
    first.cross()
    for u in range(1, 5):
        cot_units[u], cot_marks[u] = cot_unit(u, *x_pair)

    bias_units = [columns(bias[None, :], u) for u in range(5)]
    hiddens, dgs, others, biases = [], [], [], []

    def gates(u, gather, *deps):
        g, offset = place_in_group[u]
        hid, dg, db = gates_call(
            at, ids, blocks, after(own_weights[g], *deps), gather.group, offset, bias_units[u], keep, cot_units[u], sizes[u]
        )
        hiddens.append(hid[:, : reals[u]])
        dgs.append(dg)
        others.append(links.to_core(dg))
        biases.append(jnp.sum(db, axis=0).reshape(3, sizes[u])[:, : reals[u]])
        return db

    def local_gradient(units, out, offset, total, *deps):
        mine = [dgs[u] for u in units]
        mine[0] = after(mine[0], *deps)
        return weight_call(x_t, mine, [others[u] for u in units], out, offset, 3 * total)

    done = gates(0, first)
    arrived = second.waiting
    second.hop(done, *sum(cot_marks[1:], []), cross=False)
    done = gates(1, first)
    second.hops_until(hops - 2)
    second.hop(done)

    blocks_away[0] = after(blocks_away[0], done)

    if half % 16 == 0 and rows % LANES == 0:
        x_t = turn_call(at, ids, blocks + blocks_away, per_tap, half, time)
    else:
        x_t = []
        for group in (blocks, blocks_away):
            whole = jnp.zeros((time, width), BF)
            for i, block in enumerate(group):
                whole = lax.dynamic_update_slice(whole, block, (links.ids[at["time"] + i] * rows, 0))
            turned = whole.T.reshape(per_tap, 2, half, time)
            x_t.append(lax.dynamic_index_in_dim(turned, c, 1, False))
        x_t = jnp.stack(x_t)

    total = sum(sizes[:3])
    second.hop(x_t)
    second.cross()
    gates(2, second)
    done = gates(3, second)

    local = local_gradient([0, 1], None, 0, total, done)
    local = local_gradient([2], local, 3 * (sizes[0] + sizes[1]), total)
    red_first = Reduce(links, local.reshape(links.n_stream, half, -1))
    sent = red_first.hop()
    done = gates(4, second, *sent)
    sent = red_first.hops_until(hops - 2, done)

    hid = jnp.concatenate(hiddens, axis=1).reshape(n_x, own_rows, feats)
    pieces = [[own] + gather.group for own, gather in zip(own_weights, (first, second))]

    def d_inputs(k, dtype, *deps):
        now = [after(dgs[0], *deps)] + dgs[1:]
        return inputs_call(at, ids, k, now, pieces, place_in_group, own_rows, width, dtype)

    total = sum(sizes[3:])
    local = local_gradient([3], None, 0, total, *sent)
    local = local_gradient([4], local, 3 * sizes[3], total).reshape(links.n_stream, half, -1)
    red_last = Reduce(links, local)
    hid = after(hid, local)
    hid_by_k = [lax.dynamic_index_in_dim(hid, x, 0, False)]
    for k in others_x:
        hid_by_k.append(links.to_x(lax.dynamic_index_in_dim(hid, links.number("far", k), 0, False), k))
    hid = jnp.concatenate(links.in_x_order(hid_by_k), axis=1).reshape(2, rows, width)
    hid_mine = lax.dynamic_index_in_dim(hid, c, 0, False)
    hid_away = lax.dynamic_index_in_dim(hid, 1 - c, 0, False)

    sent = red_first.hop(local) + red_last.hop(local)
    d_others = [d_inputs(k, BF, *sent) for k in others_x]
    d_received = [links.to_x(a, k) for a, k in zip(d_others, others_x)]
    hid_other = links.to_core(after(hid_away, *d_others))
    hidden = jnp.stack(links.by_core(hid_mine, hid_other)).reshape(inputs.shape)
    sent = red_first.hop(*d_others, *hid_by_k[1:]) + red_last.hop(*d_others)
    d_mine = d_inputs(0, F32, *sent)

    aligned = feats % LANES == 0
    parts = [[None] * n_x for _ in sizes]

    def code(total):
        scale = jnp.maximum(jnp.max(jnp.abs(total), axis=0, keepdims=True), 1e-30) * 2.0**-15
        coded, scale = lax.optimization_barrier(((total / scale).astype(jnp.float16), scale))
        return coded, jnp.broadcast_to(scale, (8, scale.shape[1]))

    def spread(coded, scale, *deps):
        got = [(coded, scale)]
        got += [(after(links.to_x(coded, k), *deps), after(links.to_x(scale, k), *deps)) for k in others_x]
        values = [a.astype(F32) * b[:1] for a, b in got]
        return values, [links.to_core(a) for a in values]

    def put(grad_weight, units, got, crossed):
        spans = [(starts[u], sizes[u]) for u in units]
        if aligned:
            return place_call(at, ids, got + crossed, grad_weight, spans, feats, shard_rows, width)
        got = [jnp.concatenate(links.by_core(a, b), axis=0) for a, b in zip(got, crossed)]
        col = 0
        ordered = links.in_x_order(got)
        for u in units:
            for i in range(n_x):
                piece = ordered[i][:, col : col + 3 * sizes[u]]
                parts[u][i] = piece.reshape(shard_rows, 3, sizes[u])[:, :, : reals[u]]
            col += 3 * sizes[u]
        return None

    red_last.hops_until(hops - 2, d_mine)
    coded = code(red_first.total(d_mine))
    sent = red_last.hops_until(hops - 1, *d_received)
    got, crossed = spread(*coded, red_last.forth, red_last.back)
    red_last.hop()

    grad_weight = put(None, grad_members[0], got, crossed)
    for a in d_received:
        d_mine = d_mine + a.astype(F32)
    d_mine = d_mine.reshape(2, rows, width)
    d_keep = lax.dynamic_index_in_dim(d_mine, c, 0, False)
    d_other = links.to_core(lax.dynamic_index_in_dim(d_mine, 1 - c, 0, False))
    grad_inputs = jnp.stack(links.by_core(d_keep, d_other)).reshape(inputs.shape)
    red_last.forth, grad_inputs, hidden = lax.optimization_barrier((red_last.forth, grad_inputs, hidden))
    coded = code(red_last.total())

    bias_part = after(jnp.concatenate(biases, axis=1), *coded)
    bias_parts = [bias_part] + [links.to_x(bias_part, k) for k in others_x]
    bias_part = jnp.stack(links.in_x_order(bias_parts), axis=1)
    bias_part = bias_part + links.to_core(bias_part)
    bit = 1
    while bit < links.n_stream:
        swaps = [(i, i ^ bit) for i in range(links.n_stream)]
        bias_part = bias_part + lax.ppermute(bias_part, "stream", swaps)
        bit *= 2
    grad_bias = bias_part.reshape(gate_cols)

    got, crossed = spread(*coded, grad_bias, *([grad_weight] if aligned else []))
    grad_weight = put(grad_weight, grad_members[1], got, crossed)
    if not aligned:
        grad_weight = jnp.concatenate(
            [parts[u][i][:, gate] for gate in range(3) for i in range(n_x) for u in range(5)], axis=1
        )
    return (hidden, grad_inputs, grad_weight, grad_bias)


def solution(mesh):
    in_specs = (
        P(None, "stream", "stretch", None),
        P("stream", None),
        P(),
        P(None, "stream", "stretch"),
        P(None, "stream", "stretch", None),
    )
    out_specs = (
        P(None, "stream", "stretch", None),
        P(None, "stream", "stretch", None),
        P("stream", None),
        P(),
    )
    return jax.shard_map(shards, mesh=mesh, in_specs=in_specs, out_specs=out_specs, check_vma=False)
```
